256 devices in a mesh: pts: 256 (over x, y, z, core).
Axes of the slice: x: 4, y: 4, z: 8, core: 2. Of those that a mesh axis runs over, the one named last changes fastest.
Arguments:
- points: bfloat16 [262144, 256], P('pts'), may hold values from -6 to 6
- cotangent: bfloat16 [262144, 256], P('pts'), may hold values from -6 to 6
- ln1_gain: float32 [256], replicated, may hold values from 0.5 to 1.5
- w_x: bfloat16 [256, 256], replicated, may hold values from -0.375 to 0.375
- w_fx: bfloat16 [256, 256], replicated, may hold values from -0.375 to 0.375
- w_slice: float32 [32, 64], replicated, may hold values from -1 to 1
- temp_base: float32 [8], replicated, may hold values from 0.5 to 2
- ada_vec: float32 [32], replicated, may hold values from -1 to 1
- query_matrix: float32 [32, 32], replicated, may hold values from -1 to 1
- key_matrix: float32 [32, 32], replicated, may hold values from -1 to 1
- value_matrix: float32 [32, 32], replicated, may hold values from -1 to 1
- w_out: bfloat16 [256, 256], replicated, may hold values from -0.375 to 0.375
- ln2_gain: float32 [256], replicated, may hold values from 0.5 to 1.5
- w_up: bfloat16 [256, 1024], replicated, may hold values from -0.375 to 0.375
- b_up: float32 [1024], replicated, may hold values from -3 to 3
- w_down: bfloat16 [1024, 256], replicated, may hold values from -0.1875 to 0.1875
Outputs:
- grad_points: bfloat16 [262144, 256], P('pts')
- g_gain1: float32 [256], replicated
- g_x: float32 [256, 256], replicated
- g_fx: float32 [256, 256], replicated
- g_slice: float32 [32, 64], replicated
- g_base: float32 [8], replicated
- g_ada: float32 [32], replicated
- g_q: float32 [32, 32], replicated
- g_k: float32 [32, 32], replicated
- g_v: float32 [32, 32], replicated
- g_out: float32 [256, 256], replicated
- g_gain2: float32 [256], replicated
- g_up: float32 [256, 1024], replicated
- g_bup: float32 [1024], replicated
- g_down: float32 [1024, 256], replicated
The draws below stay inside these ranges and needn't reach their ends.
All inputs are finite; a program needn't handle non-finite values.
Results may differ from the reference program's by a relative error of at most 0.0066.
Values sent between devices are 32-bit elements; how exact they have to be, the bound alone decides.
A program may use at most 64 MiB of HBM per device.

```python
import math
import jax
import jax.numpy as jnp
from jax import lax

C = 256
HEADS = 8
HEAD_DIM = 32
SLICES = 64
HIDDEN_SIZE = 1024
PTS_DEV = 1024
TOKENS = 262144


def steps_of(rng, extent, cuts, least, top_value):
    def one(axis_at, parts):
        draws = jax.random.uniform(jax.random.fold_in(jax.random.fold_in(rng, 6), axis_at), (parts,), jnp.float32, least / len(cuts), top_value / len(cuts))
        return jnp.repeat(jnp.exp(draws), extent[axis_at] // parts).reshape((-1,) + (1,) * (len(extent) - axis_at - 1))

    factor_of = one(*cuts[0])
    for cut in cuts[1:]:
        factor_of = factor_of * one(*cut)
    return factor_of


def bell_draw(stream_key, dims, deviation, most, cuts=(), kind=jnp.bfloat16):
    factor_of = steps_of(stream_key, dims, cuts, -0.22, 0.18) if cuts else 1.0
    drawn = jax.random.normal(stream_key, dims, jnp.float32) * deviation * factor_of
    return jnp.minimum(jnp.maximum(drawn, -most), most).astype(kind)


def setup_inputs(seed: int = 0) -> dict:
    arg_keys = jax.random.split(jax.random.key(seed), 17)
    return {
        "points": bell_draw(arg_keys[0], (TOKENS, C), 1.0, 6.0, ((0, 256),)),
        "cotangent": bell_draw(arg_keys[1], (TOKENS, C), 1.0, 6.0, ((0, 256),)),
        "ln1_gain": jnp.clip(1.0 + 0.1 * jax.random.normal(arg_keys[2], (C,), jnp.float32), 0.5, 1.5),
        "w_x": bell_draw(arg_keys[3], (C, C), C ** -0.5, 0.375),
        "w_fx": bell_draw(arg_keys[4], (C, C), C ** -0.5, 0.375),
        "w_slice": bell_draw(arg_keys[5], (HEAD_DIM, SLICES), HEAD_DIM ** -0.5, 1.0, (), jnp.float32),
        "temp_base": jnp.clip(jnp.exp(jax.random.uniform(arg_keys[6], (HEADS,), jnp.float32, math.log(0.5), math.log(2.0))), 0.5, 2.0),
        "ada_vec": bell_draw(arg_keys[7], (HEAD_DIM,), HEAD_DIM ** -0.5, 1.0, (), jnp.float32),
        "query_matrix": bell_draw(arg_keys[8], (HEAD_DIM, HEAD_DIM), HEAD_DIM ** -0.5, 1.0, (), jnp.float32),
        "key_matrix": bell_draw(arg_keys[9], (HEAD_DIM, HEAD_DIM), HEAD_DIM ** -0.5, 1.0, (), jnp.float32),
        "value_matrix": bell_draw(arg_keys[10], (HEAD_DIM, HEAD_DIM), HEAD_DIM ** -0.5, 1.0, (), jnp.float32),
        "w_out": bell_draw(arg_keys[11], (C, C), C ** -0.5, 0.375),
        "ln2_gain": jnp.clip(1.0 + 0.1 * jax.random.normal(arg_keys[12], (C,), jnp.float32), 0.5, 1.5),
        "w_up": bell_draw(arg_keys[13], (C, HIDDEN_SIZE), C ** -0.5, 0.375),
        "b_up": bell_draw(arg_keys[14], (HIDDEN_SIZE,), 0.5, 3.0, (), jnp.float32),
        "w_down": bell_draw(arg_keys[15], (HIDDEN_SIZE, C), HIDDEN_SIZE ** -0.5, 0.1875),
    }


HIGH_INDEX = lax.Precision.HIGHEST

def layer_norm(value_rows, gain):
    centered = value_rows - lax.optimization_barrier(jnp.mean(value_rows, axis=-1, keepdims=True))
    spread = lax.optimization_barrier(jnp.mean(centered * centered, axis=-1, keepdims=True))
    return centered * lax.rsqrt(spread + 1e-05) * gain

def slice_weights(mid, w_slice, temp_base, ada_vec):
    point_count = mid.shape[0]
    split = mid.reshape(point_count, temp_base.shape[0], -1)
    tilt = jnp.tanh(jnp.einsum('phd,d->ph', split, ada_vec, precision=HIGH_INDEX))
    temper = temp_base[None, :] * jnp.exp(0.5 * tilt)
    logits = jnp.einsum('phd,dm->phm', split, w_slice, precision=HIGH_INDEX) / temper[:, :, None]
    raised = jnp.exp(logits)
    return raised / lax.optimization_barrier(jnp.sum(raised, axis=-1, keepdims=True))

def front(points, ln1_gain, w_x, w_fx, w_slice, temp_base, ada_vec):
    normed, ln_back = jax.vjp(layer_norm, points.astype(jnp.float32), ln1_gain)
    normed_b = normed.astype(jnp.bfloat16)
    mid = jnp.dot(normed_b, w_x, preferred_element_type=jnp.float32)
    feat = jnp.dot(normed_b, w_fx, preferred_element_type=jnp.float32)
    slice_weight_rows, weight_back = jax.vjp(slice_weights, mid, w_slice, temp_base, ada_vec)
    feature_head_rows = feat.reshape(slice_weight_rows.shape[0], slice_weight_rows.shape[1], -1)
    numerator_total = jnp.einsum('skn,ske->kne', slice_weight_rows, feature_head_rows, precision=HIGH_INDEX)
    denom = lax.optimization_barrier(jnp.sum(slice_weight_rows, axis=0))
    return (normed_b, ln_back, weight_back, slice_weight_rows, feature_head_rows, numerator_total, denom)

def tokens_out(numerator_total, denom, query_matrix, key_matrix, value_matrix):
    token_rows = numerator_total / (denom[:, :, None] + 1e-05)
    query_rows = jnp.einsum('lct,ty->lcy', token_rows, query_matrix, precision=HIGH_INDEX)
    key_rows = jnp.einsum('lct,ty->lcy', token_rows, key_matrix, precision=HIGH_INDEX)
    value_rows = jnp.einsum('lct,ty->lcy', token_rows, value_matrix, precision=HIGH_INDEX)
    scores = jnp.einsum('hme,hne->hmn', query_rows, key_rows, precision=HIGH_INDEX) * query_matrix.shape[0] ** (-0.5)
    raised = jnp.exp(scores)
    attn = raised / lax.optimization_barrier(jnp.sum(raised, axis=-1, keepdims=True))
    return jnp.einsum('hmn,hne->hme', attn, value_rows, precision=HIGH_INDEX)

def back_top(points, cotangent, slice_weight_rows, slice_output, ln2_gain, w_out, w_up, b_up, w_down):
    point_count = slice_weight_rows.shape[0]
    heads = slice_weight_rows.shape[1]
    blended_tokens = jnp.einsum('iwe,web->iwb', slice_weight_rows, slice_output, precision=HIGH_INDEX).reshape(point_count, -1)
    mixed_b = blended_tokens.astype(jnp.bfloat16)
    first = points.astype(jnp.float32) + jnp.dot(mixed_b, w_out, preferred_element_type=jnp.float32)
    normed, ln_back = jax.vjp(layer_norm, first, ln2_gain)
    normed_b = normed.astype(jnp.bfloat16)
    pre = jnp.dot(normed_b, w_up, preferred_element_type=jnp.float32) + b_up
    act, gelu_back = jax.vjp(jax.nn.gelu, pre)
    act_b = act.astype(jnp.bfloat16)
    g_down = jnp.einsum('pf,pc->fc', act_b, cotangent, preferred_element_type=jnp.float32)
    d_act = jnp.einsum('pc,fc->pf', cotangent, w_down, preferred_element_type=jnp.float32)
    d_pre = gelu_back(d_act)[0]
    g_bup = lax.optimization_barrier(jnp.sum(d_pre, axis=0))
    d_pre_b = d_pre.astype(jnp.bfloat16)
    g_up = jnp.einsum('pc,pf->cf', normed_b, d_pre_b, preferred_element_type=jnp.float32)
    d_normed = jnp.einsum('pf,cf->pc', d_pre_b, w_up, preferred_element_type=jnp.float32)
    d_first_ln, g_gain2 = ln_back(d_normed)
    d_first = cotangent.astype(jnp.float32) + d_first_ln
    d_first_b = d_first.astype(jnp.bfloat16)
    g_out = jnp.einsum('pk,pc->kc', mixed_b, d_first_b, preferred_element_type=jnp.float32)
    blended_gradient = jnp.einsum('pc,kc->pk', d_first_b, w_out, preferred_element_type=jnp.float32).reshape(point_count, heads, -1)
    slice_portion_gradient = jnp.einsum('skn,ske->kne', slice_weight_rows, blended_gradient, precision=HIGH_INDEX)
    weight_blend_gradient = jnp.einsum('ikl,krl->ikr', blended_gradient, slice_output, precision=HIGH_INDEX)
    return (d_first, weight_blend_gradient, slice_portion_gradient, g_gain2, g_up, g_bup, g_down, g_out)

def back_front(normed_b, ln_back, weight_back, slice_weight_rows, feature_head_rows, d_first, weight_blend_gradient, numerator_gradient, denominator_gradient, w_x, w_fx):
    point_count = slice_weight_rows.shape[0]
    weight_gradient = weight_blend_gradient + jnp.einsum('exz,iez->iex', numerator_gradient, feature_head_rows, precision=HIGH_INDEX) + denominator_gradient[None, :, :]
    feature_gradient = jnp.einsum('iwe,web->iwb', slice_weight_rows, numerator_gradient, precision=HIGH_INDEX).reshape(point_count, -1)
    d_mid, g_slice, g_base, g_ada = weight_back(weight_gradient)
    d_mid_b = d_mid.astype(jnp.bfloat16)
    d_feat_b = feature_gradient.astype(jnp.bfloat16)
    g_x = jnp.einsum('pc,pk->ck', normed_b, d_mid_b, preferred_element_type=jnp.float32)
    g_fx = jnp.einsum('pc,pk->ck', normed_b, d_feat_b, preferred_element_type=jnp.float32)
    d_normed = jnp.einsum('pk,ck->pc', d_mid_b, w_x, preferred_element_type=jnp.float32)
    d_normed = d_normed + jnp.einsum('pk,ck->pc', d_feat_b, w_fx, preferred_element_type=jnp.float32)
    d_points_ln, g_gain1 = ln_back(d_normed)
    grad_points = (d_first + d_points_ln).astype(jnp.bfloat16)
    return (grad_points, g_gain1, g_x, g_fx, g_slice, g_base, g_ada)

def reference(points, cotangent, ln1_gain, w_x, w_fx, w_slice, temp_base, ada_vec, query_matrix, key_matrix, value_matrix, w_out, ln2_gain, w_up, b_up, w_down):
    width = points.shape[1]
    blocks = points.reshape(-1, PTS_DEV, width)
    cot_blocks = cotangent.reshape(-1, PTS_DEV, width)
    front_params = (ln1_gain, w_x, w_fx, w_slice, temp_base, ada_vec)
    upper_params = (ln2_gain, w_out, w_up, b_up, w_down)
    zero_numer = jnp.zeros((HEADS, SLICES, HEAD_DIM), jnp.float32)
    zero_denom = jnp.zeros((HEADS, SLICES), jnp.float32)

    def first_pass(carry, block):
        found = front(block, *front_params)
        return ((carry[0] + found[5], carry[1] + found[6]), None)
    (numerator_total, denom), _ = lax.scan(first_pass, (zero_numer, zero_denom), blocks)
    slice_output, token_back = jax.vjp(tokens_out, numerator_total, denom, query_matrix, key_matrix, value_matrix)
    upper_init = (zero_numer, jnp.zeros((width,), jnp.float32), jnp.zeros((width, HIDDEN_SIZE), jnp.float32), jnp.zeros((HIDDEN_SIZE,), jnp.float32), jnp.zeros((HIDDEN_SIZE, width), jnp.float32), jnp.zeros((width, width), jnp.float32))

    def second_pass(carry, pair):
        found = front(pair[0], *front_params)
        upper = back_top(pair[0], pair[1], found[3], slice_output, *upper_params)
        return (tuple((a + b for a, b in zip(carry, upper[2:]))), None)
    upper_sum, _ = lax.scan(second_pass, upper_init, (blocks, cot_blocks))
    d_slice_out = upper_sum[0]
    numerator_gradient, denominator_gradient, g_q, g_k, g_v = token_back(d_slice_out)
    lower_init = (jnp.zeros((width,), jnp.float32), jnp.zeros((width, width), jnp.float32), jnp.zeros((width, width), jnp.float32), jnp.zeros((HEAD_DIM, SLICES), jnp.float32), jnp.zeros((HEADS,), jnp.float32), jnp.zeros((HEAD_DIM,), jnp.float32))

    def third_pass(carry, pair):
        found = front(pair[0], *front_params)
        upper = back_top(pair[0], pair[1], found[3], slice_output, *upper_params)
        lower = back_front(found[0], found[1], found[2], found[3], found[4], upper[0], upper[1], numerator_gradient, denominator_gradient, w_x, w_fx)
        return (tuple((a + b for a, b in zip(carry, lower[1:]))), lower[0])
    lower_sum, grads = lax.scan(third_pass, lower_init, (blocks, cot_blocks))
    grad_points = grads.reshape(-1, width)
    g_gain1, g_x, g_fx, g_slice, g_base, g_ada = lower_sum
    g_gain2, g_up, g_bup, g_down, g_out = upper_sum[1:]
    return (grad_points, g_gain1, g_x, g_fx, g_slice, g_base, g_ada, g_q, g_k, g_v, g_out, g_gain2, g_up, g_bup, g_down)
```

```python
import jax
import jax.numpy as jnp
from jax import lax
from jax.experimental import pallas as pl
from jax.experimental.pallas import tpu as pltpu
from jax.sharding import PartitionSpec as P

MESH = pl.DeviceIdType.MESH
F32 = jnp.float32
BF16 = jnp.bfloat16
C = 256
HEADS = 8
HEAD_DIM = 32
SLICES = 64
HIDDEN = 1024
LANES = HEADS * SLICES
N = 1024
TILE = 256
EPS = 1e-5
GELU_A = 0.7978845608028654
GELU_B = 0.044715

UP, DOWN, OUT = 0, 1024, 2048
WIDE = 2304
GX, GFX, REST = 0, 256, 512
TAIL = 640


def nn(a, b):
    return lax.dot_general(a, b, (((1,), (0,)), ((), ())), preferred_element_type=F32)


def nt(a, b):
    return lax.dot_general(a, b, (((1,), (1,)), ((), ())), preferred_element_type=F32)


def tn(a, b):
    return lax.dot_general(a, b, (((0,), (0,)), ((), ())), preferred_element_type=F32)


def split(x):
    hi = x.astype(BF16)
    return hi, (x - hi.astype(F32)).astype(BF16)


def exact(dot, a, b):
    ah, al = split(a)
    bh, bl = split(b)
    return dot(ah, bh) + (dot(al, bh) + dot(ah, bl))


def remote(src, dst, send_sem, recv_sem, device):
    return pltpu.make_async_remote_copy(
        src_ref=src,
        dst_ref=dst,
        send_sem=send_sem,
        recv_sem=recv_sem,
        device_id=(device,),
        device_id_type=MESH,
    )


FAR_ZC = (8, 9, 7, 10, 6, 11, 5, 12, 4, 13, 3, 14, 2, 15, 1)
FAR_XY = (10, 9, 11, 6, 14, 8, 2, 5, 7, 13, 15, 1, 3, 4, 12)
FAR_Z = (4, 3, 5, 2, 6, 1, 7)


class Place:
    def __init__(self):
        me = lax.axis_index("pts")
        self.m, self.q = lax.rem(me, 16), lax.div(me, 16)
        self.core, self.z = lax.rem(self.m, 2), lax.div(self.m, 2)

    def zc(self, d):
        return lax.rem(self.m + d, 16)

    def xy(self, d):
        return lax.rem(self.q + d, 16)

    def zc_device(self, d):
        return self.q * 16 + self.zc(d)

    def xy_device(self, d):
        return self.xy(d) * 16 + self.m

    def z_device(self, d):
        return self.q * 16 + lax.rem(self.z + d, 8) * 2 + self.core

    def other_core(self):
        return self.q * 16 + self.z * 2 + (1 - self.core)


def greet(at):
    bar = pltpu.get_barrier_semaphore()
    for d in range(1, 16):
        pl.semaphore_signal(bar, inc=1, device_id=(at.zc_device(d),), device_id_type=MESH)
        pl.semaphore_signal(bar, inc=1, device_id=(at.xy_device(d),), device_id_type=MESH)


def greeted():
    pl.semaphore_wait(pltpu.get_barrier_semaphore(), 30)


class SmallSum:
    def __init__(self, at, x, got, plane, total, sems):
        self.at, self.x, self.got, self.plane, self.total, self.sems = at, x, got, plane, total, sems
        self.sent = []

    def _start(self, copies):
        for c in copies:
            c.start()
        self.phase = copies
        self.sent += copies

    def scatter(self):
        at, s = self.at, self.sems
        self._start(
            [remote(self.x.at[at.zc(d)], self.got.at[d], s.at[0, d], s.at[1, d], at.zc_device(d)) for d in FAR_ZC]
        )

    def middle(self):
        at, s = self.at, self.sems
        for c in self.phase:
            c.wait_recv()
        part = self.x[at.m]
        for d in range(1, 16):
            part = part + self.got[d]
        self.plane[at.q] = part
        mine = self.plane.at[at.q]
        self._start([remote(mine, mine, s.at[2, d], s.at[3, d], at.xy_device(d)) for d in FAR_XY])

    def gather(self):
        at, s = self.at, self.sems
        for c in self.phase:
            c.wait_recv()
        part = self.plane[0]
        for i in range(1, 16):
            part = part + self.plane[i]
        self.total[at.m] = part
        mine = self.total.at[at.m]
        self._start([remote(mine, mine, s.at[4, d], s.at[5, d], at.zc_device(d)) for d in FAR_ZC])

    def finish(self):
        for c in self.phase:
            c.wait_recv()
        for c in self.sent:
            c.wait_send()


class WideSum:
    def __init__(self, at, x, pair, got, column, total, sems):
        self.at, self.x, self.pair, self.got, self.column = at, x, pair, got, column
        self.total, self.sems = total, sems
        self.sent = []

    def _start(self, copies):
        for c in copies:
            c.start()
        self.phase = copies
        self.sent += copies

    def _arrive(self):
        for c in self.phase:
            c.wait_recv()

    def scatter_pair(self):
        at, s = self.at, self.sems
        there = pl.ds((1 - at.core) * 16, 16)
        self._start([remote(self.x.at[there], self.pair, s.at[0, 0], s.at[1, 0], at.other_core())])

    def scatter(self):
        at, s = self.at, self.sems
        self._arrive()
        base = at.core * 16

        def add(i, _):
            self.x[base + i] += self.pair[i]
            return 0

        lax.fori_loop(0, 16, add, 0)
        self._start(
            [
                remote(self.x.at[base + at.xy(d)], self.got.at[d], s.at[2, d], s.at[3, d], at.xy_device(d))
                for d in FAR_XY
            ]
        )

    def middle(self):
        at, s = self.at, self.sems
        self._arrive()
        mine = self.x[at.core * 16 + at.q]
        for d in range(1, 16):
            mine = mine + self.got[d]
        self.column[at.z] = mine
        here = self.column.at[at.z]
        self._start([remote(here, here, s.at[4, d], s.at[5, d], at.z_device(d)) for d in FAR_Z])

    def gather(self):
        at, s = self.at, self.sems
        self._arrive()
        mine = self.column[0]
        for i in range(1, 8):
            mine = mine + self.column[i]
        slot = at.core * 16 + at.q
        self.total[slot] = mine
        here = self.total.at[slot]
        self._start([remote(here, here, s.at[6, d], s.at[7, d], at.xy_device(d)) for d in FAR_XY])

    def gather_pair(self):
        at, s = self.at, self.sems
        self._arrive()
        here = self.total.at[pl.ds(at.core * 16, 16)]
        self._start([remote(here, here, s.at[8, 0], s.at[9, 0], at.other_core())])

    def finish(self):
        self._arrive()
        for c in self.sent:
            c.wait_send()


def iota(shape, axis):
    return lax.broadcasted_iota(jnp.int32, shape, axis)


def head_mask(rows, per_row, columns, per_column):
    return iota((rows, columns), 0) // per_row == iota((rows, columns), 1) // per_column


def column_of(row):
    k = row.shape[1]
    eye = iota((k, k), 0) == iota((k, k), 1)
    return jnp.sum(jnp.where(eye, jnp.broadcast_to(row, (k, k)), 0.0), axis=1, keepdims=True)


def spread_heads(x):
    return jnp.where(head_mask(C, HEAD_DIM, LANES, SLICES), jnp.concatenate([x] * HEADS, axis=0), 0.0)


def fold_heads(x):
    x = jnp.where(head_mask(C, HEAD_DIM, LANES, SLICES), x, 0.0)
    return sum(x[h * HEAD_DIM : (h + 1) * HEAD_DIM] for h in range(HEADS))


def layer_norm(x):
    centered = x - jnp.mean(x, axis=-1, keepdims=True)
    inv = lax.rsqrt(jnp.mean(centered * centered, axis=-1, keepdims=True) + EPS)
    return centered * inv, inv


def layer_norm_back(d, hat, inv):
    a = jnp.mean(d, axis=-1, keepdims=True)
    b = jnp.mean(d * hat, axis=-1, keepdims=True)
    return inv * (d - a - hat * b)


def head_sums(x, ones):
    hi, lo = split(x)
    return jnp.concatenate(
        [nn(hi[:, k : k + 256], ones) + nn(lo[:, k : k + 256], ones) for k in (0, 256)], axis=1
    )


def kernel(
    points, cot, gain1, w_x, w_fx, w_slice, base, ada, wq, wk, wv, w_out, gain2, w_up, b_up, w_down,
    o_points, o_gx, o_gfx, o_gq, o_gk, o_gv, o_gout, o_gup, o_gdown, o_rest,
    nb, hat1, inv1, mid, feat, weight, weight_b, logits, rate, slope,
    hat2, inv2, n2b, act_b, dpre_b, dact, mixed_b, dfirst, dfirst_b, dmixed_b, dweight, dmid_b, dfeat_b, dlog_b, dtilt_b,
    ba_hi, ba_lo, ones, numer, so_b, so_l, dn_b, dn_l, denom_acc, bup_acc, gain2_acc, gain1_acc, base_acc, ada_acc, attn,
    s1_x, s1_got, s1_plane, s1_total, s2_x, s2_got, s2_plane, s2_total,
    wide_x, wide_pair, wide_got, wide_column, wide_total,
    tail_x, tail_pair, tail_got, tail_column, tail_total,
    s1_sems, s2_sems, wide_sems, tail_sems,
):
    at = Place()
    greet(at)
    first_sum = SmallSum(at, s1_x, s1_got, s1_plane, s1_total, s1_sems)
    second_sum = SmallSum(at, s2_x, s2_got, s2_plane, s2_total, s2_sems)
    wide = WideSum(at, wide_x, wide_pair, wide_got, wide_column, wide_total, wide_sems)
    tail = WideSum(at, tail_x, tail_pair, tail_got, tail_column, tail_total, tail_sems)

    ws2 = jnp.concatenate([w_slice[...]] * 2, axis=1)
    hi, lo = split(spread_heads(jnp.concatenate([ws2] * 4, axis=1)))
    ba_hi[:, :LANES], ba_lo[:, :LANES] = hi, lo
    hi, lo = split(spread_heads(jnp.broadcast_to(column_of(ada[...]), (HEAD_DIM, LANES))))
    ba_hi[:, LANES:], ba_lo[:, LANES:] = hi, lo
    ones[...] = jnp.where(head_mask(256, SLICES, 256, SLICES), 1.0, 0.0).astype(BF16)
    base_row = jnp.sum(
        jnp.where(
            iota((HEADS, LANES), 0) == iota((HEADS, LANES), 1) // SLICES,
            jnp.broadcast_to(column_of(base[...]), (HEADS, LANES)),
            0.0,
        ),
        axis=0,
        keepdims=True,
    )
    inv_base = 1.0 / base_row

    numer[...] = jnp.zeros_like(numer)
    denom_acc[...] = jnp.zeros_like(denom_acc)

    def front(i, _):
        rows = pl.ds(pl.multiple_of(i * TILE, TILE), TILE)
        hat, inv = layer_norm(points[rows].astype(F32))
        hat1[rows] = hat
        inv1[rows] = inv
        normed = (hat * gain1[...]).astype(BF16)
        nb[rows] = normed
        md = nn(normed, w_x[...])
        ft = nn(normed, w_fx[...])
        mh, ml = split(md)
        mid[rows] = mh
        lt = nn(mh, ba_hi[...]) + (nn(ml, ba_hi[...]) + nn(mh, ba_lo[...]))
        th = jnp.tanh(lt[:, LANES:])
        rt = jnp.exp(-0.5 * th) * inv_base
        rate[rows] = rt
        slope[rows] = -0.5 * (1.0 - th * th)
        lg = lt[:, :LANES] * rt
        logits[rows] = lg
        raised = jnp.exp(lg)
        w = raised / head_sums(raised, ones[...])
        weight[rows] = w
        denom_acc[...] += jnp.sum(w, axis=0, keepdims=True)
        wh, wl = split(w)
        weight_b[rows] = wh
        fh, fl = split(ft)
        feat[rows] = fh
        numer[...] += tn(fh, wh) + (tn(fl, wh) + tn(fh, wl))
        return 0

    lax.fori_loop(0, N // TILE, front, 0)

    part = fold_heads(numer[...])
    for i in range(4):
        for j in range(4):
            s1_x[i * 4 + j, :8, :] = part[8 * i : 8 * i + 8, 128 * j : 128 * j + 128]
            s1_x[i * 4 + j, 8:, :] = jnp.broadcast_to(denom_acc[:, 128 * j : 128 * j + 128], (8, 128))
    greeted()
    first_sum.scatter()

    def early(i, _):
        rows = pl.ds(pl.multiple_of(i * TILE, TILE), TILE)
        dact[rows] = nt(cot[rows], w_down[...])
        return 0

    lax.fori_loop(0, N // TILE, early, 0)
    first_sum.middle()
    first_sum.gather()
    first_sum.finish()

    numer_t = jnp.concatenate(
        [jnp.concatenate([s1_total[i * 4 + j, :8, :] for j in range(4)], axis=1) for i in range(4)], axis=0
    )
    denom = jnp.concatenate([s1_total[j, 8:9, :] for j in range(4)], axis=1) + EPS
    tok = numer_t / denom
    q_t = exact(tn, wq[...], tok)
    k_t = exact(tn, wk[...], tok)
    v_t = exact(tn, wv[...], tok)
    pair_mask = head_mask(128, SLICES, 128, SLICES)
    scale = HEAD_DIM ** (-0.5)
    outs = []
    for p in range(4):
        c = slice(128 * p, 128 * p + 128)
        e = jnp.where(pair_mask, jnp.exp(exact(tn, q_t[:, c], k_t[:, c]) * scale), 0.0)
        a = e / jnp.sum(e, axis=1, keepdims=True)
        attn[p] = a
        outs.append(exact(nt, v_t[:, c], a))
    so_b[...], so_l[...] = split(spread_heads(jnp.concatenate(outs, axis=1)))

    numer[...] = jnp.zeros_like(numer)
    bup_acc[...] = jnp.zeros_like(bup_acc)
    gain2_acc[...] = jnp.zeros_like(gain2_acc)

    def top(i, _):
        rows = pl.ds(pl.multiple_of(i * TILE, TILE), TILE)
        mb = (nt(weight_b[rows], so_b[...]) + nt(weight_b[rows], so_l[...])).astype(BF16)
        mixed_b[rows] = mb
        first = points[rows].astype(F32) + nn(mb, w_out[...])
        hat, inv = layer_norm(first)
        normed = (hat * gain2[...]).astype(BF16)
        n2b[rows] = normed
        for k in range(0, HIDDEN, 256):
            x = nn(normed, w_up[:, k : k + 256]) + b_up[:, k : k + 256]
            xx = x * x
            t = jnp.tanh(GELU_A * x * (1.0 + GELU_B * xx))
            half = 0.5 * (1.0 + t)
            act_b[rows, k : k + 256] = (x * half).astype(BF16)
            grad = half + (0.5 * GELU_A) * x * (1.0 - t * t) * (1.0 + (3.0 * GELU_B) * xx)
            d = grad * dact[rows, k : k + 256]
            bup_acc[:, k : k + 256] += jnp.sum(d, axis=0, keepdims=True)
            dpre_b[rows, k : k + 256] = d.astype(BF16)
        dn = nt(dpre_b[rows, :], w_up[...])
        gain2_acc[...] += jnp.sum(dn * hat, axis=0, keepdims=True)
        df = cot[rows].astype(F32) + layer_norm_back(dn * gain2[...], hat, inv)
        dfirst[rows] = df
        dfb = df.astype(BF16)
        dfirst_b[rows] = dfb
        dm = nt(dfb, w_out[...])
        dmh, dml = split(dm)
        dmixed_b[rows] = dmh
        wh = weight_b[rows]
        numer[...] += tn(dmh, wh) + tn(dml, wh)
        return 0

    lax.fori_loop(0, N // TILE, top, 0)

    part = fold_heads(numer[...])
    for i in range(4):
        for j in range(4):
            s2_x[i * 4 + j] = part[8 * i : 8 * i + 8, 128 * j : 128 * j + 128]
    second_sum.scatter()

    for k in range(0, HIDDEN, 256):
        wide_x[:, :, UP + k : UP + k + 256] = tn(n2b[...], dpre_b[:, k : k + 256]).reshape(32, 8, 256)
    wide_x[:, :, OUT : OUT + 256] = tn(mixed_b[...], dfirst_b[...]).reshape(32, 8, 256)
    second_sum.middle()
    for k in range(0, HIDDEN, 256):
        g = tn(act_b[:, k : k + 256], cot[...]).reshape(8, 4, 8, 256)
        for j in range(4):
            wide_x[k // 32 : k // 32 + 8, :, DOWN + 256 * j : DOWN + 256 * j + 256] = g[:, j]
    wide.scatter_pair()

    def later(i, _):
        rows = pl.ds(pl.multiple_of(i * TILE, TILE), TILE)
        dweight[rows] = nn(dmixed_b[rows], so_b[...]) + nn(dmixed_b[rows], so_l[...])
        return 0

    second_sum.gather()
    lax.fori_loop(0, N // TILE, later, 0)
    second_sum.finish()

    dso = jnp.concatenate(
        [jnp.concatenate([s2_total[i * 4 + j] for j in range(4)], axis=1) for i in range(4)], axis=0
    )
    dq, dk, dv = [], [], []
    for p in range(4):
        c = slice(128 * p, 128 * p + 128)
        a = attn[p]
        dv.append(exact(nn, dso[:, c], a))
        da = exact(tn, dso[:, c], v_t[:, c])
        ds = a * (da - jnp.sum(a * da, axis=1, keepdims=True)) * scale
        dq.append(exact(nt, k_t[:, c], ds))
        dk.append(exact(nn, q_t[:, c], ds))
    dq, dk, dv = (jnp.concatenate(v, axis=1) for v in (dq, dk, dv))
    o_gq[...] = exact(nt, tok, dq)
    o_gk[...] = exact(nt, tok, dk)
    o_gv[...] = exact(nt, tok, dv)
    dtok = exact(nn, wq[...], dq) + exact(nn, wk[...], dk) + exact(nn, wv[...], dv)
    dnumer = dtok / denom
    ddenom = -jnp.sum(dnumer * tok, axis=0, keepdims=True)
    dn_b[...], dn_l[...] = split(spread_heads(dnumer))

    gain1_acc[...] = jnp.zeros_like(gain1_acc)
    base_acc[...] = jnp.zeros_like(base_acc)
    numer[...] = jnp.zeros_like(numer)
    ada_acc[...] = jnp.zeros_like(ada_acc)

    def lower(i, _):
        rows = pl.ds(pl.multiple_of(i * TILE, TILE), TILE)
        w = weight[rows]
        dw = dweight[rows] + (nn(feat[rows], dn_b[...]) + nn(feat[rows], dn_l[...])) + ddenom
        dl = w * (dw - head_sums(w * dw, ones[...]))
        g = dl * logits[rows]
        base_acc[...] += jnp.sum(g, axis=0, keepdims=True)
        dlb = (dl * rate[rows]).astype(BF16)
        gb = (g * slope[rows]).astype(BF16)
        dlog_b[rows] = dlb
        dtilt_b[rows] = gb
        dm = nt(dlb, ba_hi[:, :LANES]) + nt(gb, ba_hi[:, LANES:])
        dmb = dm.astype(BF16)
        dmid_b[rows] = dmb
        dfb = (nt(weight_b[rows], dn_b[...]) + nt(weight_b[rows], dn_l[...])).astype(BF16)
        dfeat_b[rows] = dfb
        mh = mid[rows]
        numer[...] += tn(mh, dlb)
        ada_acc[...] += tn(mh, gb)
        dn = nt(dmb, w_x[...]) + nt(dfb, w_fx[...])
        hat = hat1[rows]
        gain1_acc[...] += jnp.sum(dn * hat, axis=0, keepdims=True)
        o_points[rows] = (dfirst[rows] + layer_norm_back(dn * gain1[...], hat, inv1[rows])).astype(BF16)
        return 0

    wide.scatter()
    lax.fori_loop(0, N // TILE, lower, 0)
    wide.middle()
    tail_x[:, :, GX : GX + 256] = tn(nb[...], dmid_b[...]).reshape(32, 8, 256)
    tail_x[:, :, GFX : GFX + 256] = tn(nb[...], dfeat_b[...]).reshape(32, 8, 256)
    gs = fold_heads(numer[...])
    ga = fold_heads(ada_acc[...])
    gs = (gs[:, :128] + gs[:, 128:256]) + (gs[:, 256:384] + gs[:, 384:])
    ga = (ga[:, :128] + ga[:, 128:256]) + (ga[:, 256:384] + ga[:, 384:])
    rest = (REST, REST + 128)
    tail_x[:, :, REST : REST + 128] = jnp.zeros((32, 8, 128), F32)
    tail_x[0:4, :, REST : REST + 128] = gs.reshape(4, 8, 128)
    tail_x[4:8, :, REST : REST + 128] = ga.reshape(4, 8, 128)
    for i in range(8):
        tail_x[8, i : i + 1, rest[0] : rest[1]] = bup_acc[:, 128 * i : 128 * i + 128]
    for i in range(4):
        tail_x[9, i : i + 1, rest[0] : rest[1]] = base_acc[:, 128 * i : 128 * i + 128]
    for i in range(2):
        tail_x[10, i : i + 1, rest[0] : rest[1]] = gain1_acc[:, 128 * i : 128 * i + 128]
        tail_x[10, i + 2 : i + 3, rest[0] : rest[1]] = gain2_acc[:, 128 * i : 128 * i + 128]
    tail.scatter_pair()
    tail.scatter()
    wide.gather()
    tail.middle()
    tail.gather()
    wide.gather_pair()
    tail.gather_pair()
    wide.finish()
    tail.finish()
    o_gup[...] = wide_total[:, :, UP : UP + 1024]
    for j in range(4):
        o_gdown[:, j] = wide_total[:, :, DOWN + 256 * j : DOWN + 256 * j + 256]
    o_gout[...] = wide_total[:, :, OUT : OUT + 256]
    o_gx[...] = tail_total[:, :, GX : GX + 256]
    o_gfx[...] = tail_total[:, :, GFX : GFX + 256]

    o_rest[...] = jnp.zeros_like(o_rest)
    gs = tail_total[0:4, :, rest[0] : rest[1]].reshape(32, 128)
    o_rest[0:32, :] = gs + pltpu.roll(gs, 64, 1)
    ga = tail_total[4:8, :, rest[0] : rest[1]].reshape(32, 128)
    ga = jnp.sum(ga, axis=1, keepdims=True)
    o_rest[32:33, 0:32] = jnp.sum(
        jnp.where(iota((32, 32), 0) == iota((32, 32), 1), jnp.broadcast_to(ga, (32, 32)), 0.0), axis=0, keepdims=True
    )
    gb = jnp.concatenate([tail_total[9, i : i + 1, rest[0] : rest[1]] for i in range(4)], axis=1)
    gb = gb * (-inv_base)
    pick = iota((HEADS, LANES), 0) == iota((HEADS, LANES), 1) // SLICES
    gb = jnp.sum(jnp.where(pick, jnp.broadcast_to(gb, (HEADS, LANES)), 0.0), axis=1, keepdims=True)
    o_rest[33:34, 0:8] = jnp.sum(
        jnp.where(iota((8, 8), 0) == iota((8, 8), 1), jnp.broadcast_to(gb, (8, 8)), 0.0), axis=0, keepdims=True
    )
    o_rest[34:38, :] = tail_total[10, 0:4, rest[0] : rest[1]]
    o_rest[40:48, :] = tail_total[8, :, rest[0] : rest[1]]


def per_device(*args):
    (points, cot, gain1, w_x, w_fx, w_slice, base, ada, wq, wk, wv, w_out, gain2, w_up, b_up, w_down) = args
    row = lambda v: v.reshape(1, -1)
    ins = (
        points, cot, row(gain1), w_x, w_fx, w_slice, row(base), row(ada), wq, wk, wv, w_out, row(gain2), w_up,
        row(b_up), w_down,
    )
    spec = pl.BlockSpec(memory_space=pltpu.VMEM)
    outs = [
        ((N, C), BF16),
        ((32, 8, 256), F32),
        ((32, 8, 256), F32),
        ((32, 32), F32),
        ((32, 32), F32),
        ((32, 32), F32),
        ((32, 8, 256), F32),
        ((32, 8, 1024), F32),
        ((32, 4, 8, 256), F32),
        ((48, 128), F32),
    ]
    held = [
        ((N, C), BF16), ((N, C), F32), ((N, 1), F32), ((N, C), BF16), ((N, C), BF16), ((N, LANES), F32),
        ((N, LANES), BF16), ((N, LANES), F32), ((N, LANES), F32), ((N, LANES), F32),
        ((8, C), F32), ((8, 1), F32), ((N, C), BF16), ((N, HIDDEN), BF16), ((N, HIDDEN), BF16), ((N, HIDDEN), F32),
        ((N, C), BF16), ((N, C), F32), ((N, C), BF16), ((N, C), BF16), ((N, LANES), F32), ((N, C), BF16),
        ((N, C), BF16), ((N, LANES), BF16), ((N, LANES), BF16),
        ((C, 2 * LANES), BF16), ((C, 2 * LANES), BF16), ((256, 256), BF16), ((C, LANES), F32), ((C, LANES), BF16), ((C, LANES), BF16),
        ((C, LANES), BF16), ((C, LANES), BF16), ((1, LANES), F32), ((1, HIDDEN), F32), ((1, C), F32), ((1, C), F32), ((1, LANES), F32),
        ((C, LANES), F32), ((4, 128, 128), F32),
        *(((16, 16, 128), F32),) * 4, *(((16, 8, 128), F32),) * 4,
        ((32, 8, WIDE), F32), ((16, 8, WIDE), F32), ((16, 8, WIDE), F32), ((8, 8, WIDE), F32), ((32, 8, WIDE), F32),
        ((32, 8, TAIL), F32), ((16, 8, TAIL), F32), ((16, 8, TAIL), F32), ((8, 8, TAIL), F32), ((32, 8, TAIL), F32),
    ]
    sems = [pltpu.SemaphoreType.DMA((k, 16)) for k in (6, 6, 10, 10)]
    got = pl.pallas_call(
        kernel,
        out_shape=[jax.ShapeDtypeStruct(s, d) for s, d in outs],
        in_specs=[spec] * len(ins),
        out_specs=[spec] * len(outs),
        scratch_shapes=[pltpu.VMEM(s, d) for s, d in held] + sems,
        compiler_params=pltpu.CompilerParams(
            collective_id=1, has_side_effects=True, vmem_limit_bytes=60 << 20
        ),
    )(*ins)
    g_points, g_x, g_fx, g_q, g_k, g_v, g_out, g_up, g_down, rest = got
    return (
        g_points,
        rest[34:36].reshape(C),
        g_x.reshape(C, C),
        g_fx.reshape(C, C),
        rest[0:32, 0:SLICES],
        rest[33, 0:HEADS],
        rest[32, 0:HEAD_DIM],
        g_q,
        g_k,
        g_v,
        g_out.reshape(C, C),
        rest[36:38].reshape(C),
        g_up.reshape(C, HIDDEN),
        rest[40:48].reshape(HIDDEN),
        g_down.reshape(HIDDEN, C),
    )


def solution(mesh):
    rows, whole = P("pts", None), P()
    return jax.shard_map(
        per_device,
        mesh=mesh,
        in_specs=(rows, rows) + (whole,) * 14,
        out_specs=(rows,) + (whole,) * 14,
        check_vma=False,
    )
```

```python
import jax
import jax.numpy as jnp
from jax import lax
from jax.experimental import pallas as pl
from jax.experimental.pallas import tpu as pltpu
from jax.sharding import PartitionSpec as P

MESH = pl.DeviceIdType.MESH
F32 = jnp.float32
BF16 = jnp.bfloat16
C = 256
HEADS = 8
HEAD_DIM = 32
SLICES = 64
HIDDEN = 1024
LANES = HEADS * SLICES
N = 1024
TILE = 256
EPS = 1e-5
GELU_A = 0.7978845608028654
GELU_B = 0.044715

UP, DOWN_A, WIDE_A = 0, 1024, 1536
DOWN_B, OUT, WIDE_B = 0, 512, 768
GX, GFX, REST = 0, 256, 512
TAIL = 640


def nn(a, b):
    return lax.dot_general(a, b, (((1,), (0,)), ((), ())), preferred_element_type=F32)


def nt(a, b):
    return lax.dot_general(a, b, (((1,), (1,)), ((), ())), preferred_element_type=F32)


def tn(a, b):
    return lax.dot_general(a, b, (((0,), (0,)), ((), ())), preferred_element_type=F32)


def split(x):
    hi = x.astype(BF16)
    return hi, (x - hi.astype(F32)).astype(BF16)


def exact(dot, a, b):
    ah, al = split(a)
    bh, bl = split(b)
    return dot(ah, bh) + (dot(al, bh) + dot(ah, bl))


def remote(src, dst, send_sem, recv_sem, device):
    return pltpu.make_async_remote_copy(
        src_ref=src,
        dst_ref=dst,
        send_sem=send_sem,
        recv_sem=recv_sem,
        device_id=(device,),
        device_id_type=MESH,
    )


FAR_ZC = (8, 9, 7, 10, 6, 11, 5, 12, 4, 13, 3, 14, 2, 15, 1)
FAR_XY = (10, 9, 11, 6, 14, 8, 2, 5, 7, 13, 15, 1, 3, 4, 12)
FAR_Z = (4, 3, 5, 2, 6, 1, 7)


class Place:
    def __init__(self):
        me = lax.axis_index("pts")
        self.m, self.q = lax.rem(me, 16), lax.div(me, 16)
        self.core, self.z = lax.rem(self.m, 2), lax.div(self.m, 2)

    def zc(self, d):
        return lax.rem(self.m + d, 16)

    def xy(self, d):
        return lax.rem(self.q + d, 16)

    def zc_device(self, d):
        return self.q * 16 + self.zc(d)

    def xy_device(self, d):
        return self.xy(d) * 16 + self.m

    def z_device(self, d):
        return self.q * 16 + lax.rem(self.z + d, 8) * 2 + self.core

    def other_core(self):
        return self.q * 16 + self.z * 2 + (1 - self.core)


def greet(at):
    bar = pltpu.get_barrier_semaphore()
    for d in range(1, 16):
        pl.semaphore_signal(bar, inc=1, device_id=(at.zc_device(d),), device_id_type=MESH)
        pl.semaphore_signal(bar, inc=1, device_id=(at.xy_device(d),), device_id_type=MESH)


def greeted():
    pl.semaphore_wait(pltpu.get_barrier_semaphore(), 30)


class SmallSum:
    def __init__(self, at, x, got, plane, total, sems):
        self.at, self.x, self.got, self.plane, self.total, self.sems = at, x, got, plane, total, sems
        self.sent = []

    def _start(self, copies):
        for c in copies:
            c.start()
        self.phase = copies
        self.sent += copies

    def scatter(self):
        at, s = self.at, self.sems
        self._start(
            [remote(self.x.at[at.zc(d)], self.got.at[d], s.at[0, d], s.at[1, d], at.zc_device(d)) for d in FAR_ZC]
        )

    def middle(self):
        at, s = self.at, self.sems
        for c in self.phase:
            c.wait_recv()
        part = self.x[at.m]
        for d in range(1, 16):
            part = part + self.got[d]
        self.plane[at.q] = part
        mine = self.plane.at[at.q]
        self._start([remote(mine, mine, s.at[2, d], s.at[3, d], at.xy_device(d)) for d in FAR_XY])

    def gather(self):
        at, s = self.at, self.sems
        for c in self.phase:
            c.wait_recv()
        part = self.plane[0]
        for i in range(1, 16):
            part = part + self.plane[i]
        self.total[at.m] = part
        mine = self.total.at[at.m]
        self._start([remote(mine, mine, s.at[4, d], s.at[5, d], at.zc_device(d)) for d in FAR_ZC])

    def finish(self):
        for c in self.phase:
            c.wait_recv()
        for c in self.sent:
            c.wait_send()


class WideSum:
    def __init__(self, at, z_first, x, pair, got, column, total, sems):
        self.at, self.x, self.pair, self.got, self.column = at, x, pair, got, column
        self.total, self.sems = total, sems
        plane = (FAR_XY, at.q, at.xy, at.xy_device)
        line = (FAR_Z, at.z, lambda d: lax.rem(at.z + d, 8), at.z_device)
        self.first, self.second = (line, plane) if z_first else (plane, line)
        self.per = got.shape[1]
        self.sent = []

    def _slabs(self, index):
        return pl.ds(self.at.core * 16 + index * self.per, self.per)

    def _start(self, copies):
        for c in copies:
            c.start()
        self.phase = copies
        self.sent += copies

    def _arrive(self):
        for c in self.phase:
            c.wait_recv()

    def scatter_pair(self):
        at, s = self.at, self.sems
        there = pl.ds((1 - at.core) * 16, 16)
        self._start([remote(self.x.at[there], self.pair, s.at[0, 0], s.at[1, 0], at.other_core())])

    def scatter(self):
        s = self.sems
        self._arrive()
        base = self.at.core * 16

        def add(i, _):
            self.x[base + i] += self.pair[i]
            return 0

        lax.fori_loop(0, 16, add, 0)
        far, _, index, device = self.first
        self._start(
            [
                remote(self.x.at[self._slabs(index(d))], self.got.at[d], s.at[2, d], s.at[3, d], device(d))
                for d in far
            ]
        )

    def middle(self):
        s = self.sems
        self._arrive()
        mine = self.x[self._slabs(self.first[1])]
        for d in range(1, self.got.shape[0]):
            mine = mine + self.got[d]
        far, own, _, device = self.second
        self.column[own] = mine
        here = self.column.at[own]
        self._start([remote(here, here, s.at[4, d], s.at[5, d], device(d)) for d in far])

    def gather(self):
        s = self.sems
        self._arrive()
        mine = self.column[0]
        for i in range(1, self.column.shape[0]):
            mine = mine + self.column[i]
        far, own, _, device = self.first
        slabs = self._slabs(own)
        self.total[slabs] = mine
        here = self.total.at[slabs]
        self._start([remote(here, here, s.at[6, d], s.at[7, d], device(d)) for d in far])

    def gather_pair(self):
        at, s = self.at, self.sems
        self._arrive()
        here = self.total.at[pl.ds(at.core * 16, 16)]
        self._start([remote(here, here, s.at[8, 0], s.at[9, 0], at.other_core())])

    def finish(self):
        self._arrive()
        for c in self.sent:
            c.wait_send()


def iota(shape, axis):
    return lax.broadcasted_iota(jnp.int32, shape, axis)


def head_mask(rows, per_row, columns, per_column):
    return iota((rows, columns), 0) // per_row == iota((rows, columns), 1) // per_column


def column_of(row):
    k = row.shape[1]
    eye = iota((k, k), 0) == iota((k, k), 1)
    return jnp.sum(jnp.where(eye, jnp.broadcast_to(row, (k, k)), 0.0), axis=1, keepdims=True)


def row_of(column):
    k = column.shape[0]
    eye = iota((k, k), 0) == iota((k, k), 1)
    return jnp.sum(jnp.where(eye, jnp.broadcast_to(column, (k, k)), 0.0), axis=0, keepdims=True)


def spread_heads(x):
    return jnp.where(head_mask(C, HEAD_DIM, LANES, SLICES), jnp.concatenate([x] * HEADS, axis=0), 0.0)


def fold_heads(x):
    x = jnp.where(head_mask(C, HEAD_DIM, LANES, SLICES), x, 0.0)
    return sum(x[h * HEAD_DIM : (h + 1) * HEAD_DIM] for h in range(HEADS))


def layer_norm(x):
    centered = x - jnp.mean(x, axis=-1, keepdims=True)
    inv = lax.rsqrt(jnp.mean(centered * centered, axis=-1, keepdims=True) + EPS)
    return centered * inv, inv


def layer_norm_back(d, hat, inv):
    a = jnp.mean(d, axis=-1, keepdims=True)
    b = jnp.mean(d * hat, axis=-1, keepdims=True)
    return inv * (d - a - hat * b)


def head_sums(x, ones):
    hi, lo = split(x)
    return jnp.concatenate(
        [nn(hi[:, k : k + 256], ones) + nn(lo[:, k : k + 256], ones) for k in (0, 256)], axis=1
    )


def kernel(
    points, cot, gain1, w_x, w_fx, w_slice, base, ada, wq, wk, wv, w_out, gain2, w_up, b_up, w_down,
    o_points, o_ggain1, o_gx, o_gfx, o_gslice, o_gbase, o_gada, o_gq, o_gk, o_gv, o_gout, o_ggain2, o_gup, o_gbup, o_gdown,
    nb, hat1, inv1, mid, feat, weight, weight_b, logits, rate, slope,
    hat2, inv2, n2b, act_b, dpre_b, dact, mixed_b, dfirst, dfirst_b, dmixed_b, dweight, dmid_b, dfeat_b, dlog_b, dtilt_b,
    ba_hi, ba_lo, ones, numer, so_b, so_l, dn_b, dn_l, denom_acc, bup_acc, gain2_acc, gain1_acc, base_acc, ada_acc, attn,
    s1_x, s1_got, s1_plane, s1_total, s2_x, s2_got, s2_plane, s2_total,
    a_x, a_pair, a_got, a_column, a_total,
    b_x, b_pair, b_got, b_column, b_total,
    tail_x, tail_pair, tail_got, tail_column, tail_total,
    s1_sems, s2_sems, a_sems, b_sems, tail_sems, out_sems, points_out,
):
    at = Place()
    greet(at)
    first_sum = SmallSum(at, s1_x, s1_got, s1_plane, s1_total, s1_sems)
    second_sum = SmallSum(at, s2_x, s2_got, s2_plane, s2_total, s2_sems)
    wide_a = WideSum(at, False, a_x, a_pair, a_got, a_column, a_total, a_sems)
    wide_b = WideSum(at, True, b_x, b_pair, b_got, b_column, b_total, b_sems)
    tail = WideSum(at, False, tail_x, tail_pair, tail_got, tail_column, tail_total, tail_sems)

    ws2 = jnp.concatenate([w_slice[...]] * 2, axis=1)
    hi, lo = split(spread_heads(jnp.concatenate([ws2] * 4, axis=1)))
    ba_hi[:, :LANES], ba_lo[:, :LANES] = hi, lo
    hi, lo = split(spread_heads(jnp.broadcast_to(column_of(ada[...]), (HEAD_DIM, LANES))))
    ba_hi[:, LANES:], ba_lo[:, LANES:] = hi, lo
    ones[...] = jnp.where(head_mask(256, SLICES, 256, SLICES), 1.0, 0.0).astype(BF16)
    base_row = jnp.sum(
        jnp.where(
            iota((HEADS, LANES), 0) == iota((HEADS, LANES), 1) // SLICES,
            jnp.broadcast_to(column_of(base[...]), (HEADS, LANES)),
            0.0,
        ),
        axis=0,
        keepdims=True,
    )
    inv_base = 1.0 / base_row

    numer[...] = jnp.zeros_like(numer)
    denom_acc[...] = jnp.zeros_like(denom_acc)

    def front(i, _):
        rows = pl.ds(pl.multiple_of(i * TILE, TILE), TILE)
        hat, inv = layer_norm(points[rows].astype(F32))
        hat1[rows] = hat
        inv1[rows] = inv
        normed = (hat * gain1[...]).astype(BF16)
        nb[rows] = normed
        md = nn(normed, w_x[...])
        ft = nn(normed, w_fx[...])
        mh, ml = split(md)
        mid[rows] = mh
        lt = nn(mh, ba_hi[...]) + (nn(ml, ba_hi[...]) + nn(mh, ba_lo[...]))
        th = jnp.tanh(lt[:, LANES:])
        rt = jnp.exp(-0.5 * th) * inv_base
        rate[rows] = rt
        slope[rows] = -0.5 * (1.0 - th * th)
        lg = lt[:, :LANES] * rt
        logits[rows] = lg
        raised = jnp.exp(lg)
        w = raised / head_sums(raised, ones[...])
        weight[rows] = w
        denom_acc[...] += jnp.sum(w, axis=0, keepdims=True)
        wh, wl = split(w)
        weight_b[rows] = wh
        fh, fl = split(ft)
        feat[rows] = fh
        numer[...] += tn(fh, wh) + (tn(fl, wh) + tn(fh, wl))
        return 0

    lax.fori_loop(0, N // TILE, front, 0)

    part = fold_heads(numer[...])
    for i in range(4):
        for j in range(4):
            s1_x[i * 4 + j, :8, :] = part[8 * i : 8 * i + 8, 128 * j : 128 * j + 128]
            s1_x[i * 4 + j, 8:, :] = jnp.broadcast_to(denom_acc[:, 128 * j : 128 * j + 128], (8, 128))
    greeted()
    first_sum.scatter()

    def early(i, _):
        rows = pl.ds(pl.multiple_of(i * TILE, TILE), TILE)
        dact[rows] = nt(cot[rows], w_down[...])
        return 0

    lax.fori_loop(0, N // TILE, early, 0)
    first_sum.middle()
    first_sum.gather()
    first_sum.finish()

    numer_t = jnp.concatenate(
        [jnp.concatenate([s1_total[i * 4 + j, :8, :] for j in range(4)], axis=1) for i in range(4)], axis=0
    )
    denom = jnp.concatenate([s1_total[j, 8:9, :] for j in range(4)], axis=1) + EPS
    tok = numer_t / denom
    q_t = exact(tn, wq[...], tok)
    k_t = exact(tn, wk[...], tok)
    v_t = exact(tn, wv[...], tok)
    pair_mask = head_mask(128, SLICES, 128, SLICES)
    scale = HEAD_DIM ** (-0.5)
    outs = []
    for p in range(4):
        c = slice(128 * p, 128 * p + 128)
        e = jnp.where(pair_mask, jnp.exp(exact(tn, q_t[:, c], k_t[:, c]) * scale), 0.0)
        a = e / jnp.sum(e, axis=1, keepdims=True)
        attn[p] = a
        outs.append(exact(nt, v_t[:, c], a))
    so_b[...], so_l[...] = split(spread_heads(jnp.concatenate(outs, axis=1)))

    numer[...] = jnp.zeros_like(numer)
    bup_acc[...] = jnp.zeros_like(bup_acc)
    gain2_acc[...] = jnp.zeros_like(gain2_acc)

    def top(i, _):
        rows = pl.ds(pl.multiple_of(i * TILE, TILE), TILE)
        mb = (nt(weight_b[rows], so_b[...]) + nt(weight_b[rows], so_l[...])).astype(BF16)
        mixed_b[rows] = mb
        first = points[rows].astype(F32) + nn(mb, w_out[...])
        hat, inv = layer_norm(first)
        normed = (hat * gain2[...]).astype(BF16)
        n2b[rows] = normed
        for k in range(0, HIDDEN, 256):
            x = nn(normed, w_up[:, k : k + 256]) + b_up[:, k : k + 256]
            xx = x * x
            t = jnp.tanh(GELU_A * x * (1.0 + GELU_B * xx))
            half = 0.5 * (1.0 + t)
            act_b[rows, k : k + 256] = (x * half).astype(BF16)
            grad = half + (0.5 * GELU_A) * x * (1.0 - t * t) * (1.0 + (3.0 * GELU_B) * xx)
            d = grad * dact[rows, k : k + 256]
            bup_acc[:, k : k + 256] += jnp.sum(d, axis=0, keepdims=True)
            dpre_b[rows, k : k + 256] = d.astype(BF16)
        dn = nt(dpre_b[rows, :], w_up[...])
        gain2_acc[...] += jnp.sum(dn * hat, axis=0, keepdims=True)
        df = cot[rows].astype(F32) + layer_norm_back(dn * gain2[...], hat, inv)
        dfirst[rows] = df
        dfb = df.astype(BF16)
        dfirst_b[rows] = dfb
        dm = nt(dfb, w_out[...])
        dmh, dml = split(dm)
        dmixed_b[rows] = dmh
        wh = weight_b[rows]
        numer[...] += tn(dmh, wh) + tn(dml, wh)
        return 0

    lax.fori_loop(0, N // TILE, top, 0)

    part = fold_heads(numer[...])
    for i in range(4):
        for j in range(4):
            s2_x[i * 4 + j] = part[8 * i : 8 * i + 8, 128 * j : 128 * j + 128]
    second_sum.scatter()

    for k in range(0, HIDDEN, 256):
        a_x[:, :, UP + k : UP + k + 256] = tn(n2b[...], dpre_b[:, k : k + 256]).reshape(32, 8, 256)
    b_x[:, :, OUT : OUT + 256] = tn(mixed_b[...], dfirst_b[...]).reshape(32, 8, 256)
    second_sum.middle()
    for k in range(0, HIDDEN, 256):
        g = tn(act_b[:, k : k + 256], cot[...]).reshape(8, 4, 8, 256)
        for j in range(2):
            a_x[k // 32 : k // 32 + 8, :, DOWN_A + 256 * j : DOWN_A + 256 * j + 256] = g[:, j]
            b_x[k // 32 : k // 32 + 8, :, DOWN_B + 256 * j : DOWN_B + 256 * j + 256] = g[:, j + 2]
    wide_a.scatter_pair()
    wide_b.scatter_pair()

    def later(i, _):
        rows = pl.ds(pl.multiple_of(i * TILE, TILE), TILE)
        dweight[rows] = nn(dmixed_b[rows], so_b[...]) + nn(dmixed_b[rows], so_l[...])
        return 0

    second_sum.gather()
    wide_a.scatter()
    lax.fori_loop(0, N // TILE, later, 0)
    second_sum.finish()
    wide_b.scatter()

    dso = jnp.concatenate(
        [jnp.concatenate([s2_total[i * 4 + j] for j in range(4)], axis=1) for i in range(4)], axis=0
    )
    dq, dk, dv = [], [], []
    for p in range(4):
        c = slice(128 * p, 128 * p + 128)
        a = attn[p]
        dv.append(exact(nn, dso[:, c], a))
        da = exact(tn, dso[:, c], v_t[:, c])
        ds = a * (da - jnp.sum(a * da, axis=1, keepdims=True)) * scale
        dq.append(exact(nt, k_t[:, c], ds))
        dk.append(exact(nn, q_t[:, c], ds))
    dq, dk, dv = (jnp.concatenate(v, axis=1) for v in (dq, dk, dv))
    o_gq[...] = exact(nt, tok, dq)
    o_gk[...] = exact(nt, tok, dk)
    o_gv[...] = exact(nt, tok, dv)
    dtok = exact(nn, wq[...], dq) + exact(nn, wk[...], dk) + exact(nn, wv[...], dv)
    dnumer = dtok / denom
    ddenom = -jnp.sum(dnumer * tok, axis=0, keepdims=True)
    dn_b[...], dn_l[...] = split(spread_heads(dnumer))

    gain1_acc[...] = jnp.zeros_like(gain1_acc)
    base_acc[...] = jnp.zeros_like(base_acc)
    numer[...] = jnp.zeros_like(numer)
    ada_acc[...] = jnp.zeros_like(ada_acc)

    def lower(i, _):
        rows = pl.ds(pl.multiple_of(i * TILE, TILE), TILE)
        w = weight[rows]
        dw = dweight[rows] + (nn(feat[rows], dn_b[...]) + nn(feat[rows], dn_l[...])) + ddenom
        dl = w * (dw - head_sums(w * dw, ones[...]))
        g = dl * logits[rows]
        base_acc[...] += jnp.sum(g, axis=0, keepdims=True)
        dlb = (dl * rate[rows]).astype(BF16)
        gb = (g * slope[rows]).astype(BF16)
        dlog_b[rows] = dlb
        dtilt_b[rows] = gb
        dm = nt(dlb, ba_hi[:, :LANES]) + nt(gb, ba_hi[:, LANES:])
        dmb = dm.astype(BF16)
        dmid_b[rows] = dmb
        dfb = (nt(weight_b[rows], dn_b[...]) + nt(weight_b[rows], dn_l[...])).astype(BF16)
        dfeat_b[rows] = dfb
        mh = mid[rows]
        numer[...] += tn(mh, dlb)
        ada_acc[...] += tn(mh, gb)
        dn = nt(dmb, w_x[...]) + nt(dfb, w_fx[...])
        hat = hat1[rows]
        gain1_acc[...] += jnp.sum(dn * hat, axis=0, keepdims=True)
        points_out[rows] = (dfirst[rows] + layer_norm_back(dn * gain1[...], hat, inv1[rows])).astype(BF16)
        return 0

    lax.fori_loop(0, N // TILE, lower, 0)
    leaving = [pltpu.make_async_copy(points_out, o_points, out_sems.at[0])]
    leaving[0].start()
    wide_a.middle()
    wide_b.middle()
    tail_x[:, :, GX : GX + 256] = tn(nb[...], dmid_b[...]).reshape(32, 8, 256)
    tail_x[:, :, GFX : GFX + 256] = tn(nb[...], dfeat_b[...]).reshape(32, 8, 256)
    gs = fold_heads(numer[...])
    ga = fold_heads(ada_acc[...])
    gs = (gs[:, :128] + gs[:, 128:256]) + (gs[:, 256:384] + gs[:, 384:])
    ga = (ga[:, :128] + ga[:, 128:256]) + (ga[:, 256:384] + ga[:, 384:])
    rest = (REST, REST + 128)
    tail_x[:, :, REST : REST + 128] = jnp.zeros((32, 8, 128), F32)
    tail_x[0:4, :, REST : REST + 128] = gs.reshape(4, 8, 128)
    tail_x[4:8, :, REST : REST + 128] = ga.reshape(4, 8, 128)
    for i in range(8):
        tail_x[8, i : i + 1, rest[0] : rest[1]] = bup_acc[:, 128 * i : 128 * i + 128]
    for i in range(4):
        tail_x[9, i : i + 1, rest[0] : rest[1]] = base_acc[:, 128 * i : 128 * i + 128]
    for i in range(2):
        tail_x[10, i : i + 1, rest[0] : rest[1]] = gain1_acc[:, 128 * i : 128 * i + 128]
        tail_x[10, i + 2 : i + 3, rest[0] : rest[1]] = gain2_acc[:, 128 * i : 128 * i + 128]
    tail.scatter_pair()
    tail.scatter()
    wide_a.gather()
    wide_b.gather()
    tail.middle()
    tail.gather()
    wide_a.gather_pair()
    wide_b.gather_pair()
    tail.gather_pair()
    wide_a.finish()
    wide_b.finish()
    tail.finish()
    def leave(src, dst):
        c = pltpu.make_async_copy(src, dst, out_sems.at[len(leaving)])
        c.start()
        leaving.append(c)

    leave(a_total.at[:, :, UP : UP + 1024], o_gup)
    for j in range(2):
        leave(a_total.at[:, :, DOWN_A + 256 * j : DOWN_A + 256 * j + 256], o_gdown.at[:, j])
        leave(b_total.at[:, :, DOWN_B + 256 * j : DOWN_B + 256 * j + 256], o_gdown.at[:, j + 2])
    leave(b_total.at[:, :, OUT : OUT + 256], o_gout)
    leave(tail_total.at[:, :, GX : GX + 256], o_gx)
    leave(tail_total.at[:, :, GFX : GFX + 256], o_gfx)

    gs = tail_total[0:4, :, rest[0] : rest[1]].reshape(32, 128)
    o_gslice[...] = (gs + pltpu.roll(gs, SLICES, 1))[:, :SLICES]
    ga = tail_total[4:8, :, rest[0] : rest[1]].reshape(32, 128)
    o_gada[...] = row_of(jnp.sum(ga, axis=1, keepdims=True))
    gb = jnp.concatenate([tail_total[9, i : i + 1, rest[0] : rest[1]] for i in range(4)], axis=1)
    gb = gb * (-inv_base)
    pick = iota((HEADS, LANES), 0) == iota((HEADS, LANES), 1) // SLICES
    gb = jnp.sum(jnp.where(pick, jnp.broadcast_to(gb, (HEADS, LANES)), 0.0), axis=1, keepdims=True)
    o_gbase[...] = row_of(gb)
    for i in range(2):
        o_ggain1[:, 128 * i : 128 * i + 128] = tail_total[10, i : i + 1, rest[0] : rest[1]]
        o_ggain2[:, 128 * i : 128 * i + 128] = tail_total[10, i + 2 : i + 3, rest[0] : rest[1]]
    for i in range(8):
        o_gbup[:, 128 * i : 128 * i + 128] = tail_total[8, i : i + 1, rest[0] : rest[1]]
    for c in leaving:
        c.wait()


def write_out(*refs):
    sems = refs[-1]
    count = (len(refs) - 1) // 2
    copies = [pltpu.make_async_copy(refs[i], refs[count + i], sems.at[i]) for i in range(count)]
    for c in copies:
        c.start()
    for c in copies:
        c.wait()


def wide_buffers(columns, first, second, per):
    return [
        (shape + (8, columns), F32) for shape in ((32,), (16,), (first, per), (second, per), (32,))
    ]


def per_device(*args):
    (points, cot, gain1, w_x, w_fx, w_slice, base, ada, wq, wk, wv, w_out, gain2, w_up, b_up, w_down) = args
    row = lambda v: v.reshape(1, -1)
    ins = (
        points, cot, row(gain1), w_x, w_fx, w_slice, row(base), row(ada), wq, wk, wv, w_out, row(gain2), w_up,
        row(b_up), w_down,
    )
    spec = pl.BlockSpec(memory_space=pltpu.VMEM)
    outs = [
        ((N, C), BF16), ((1, C), F32), ((32, 8, 256), F32), ((32, 8, 256), F32), ((HEAD_DIM, SLICES), F32),
        ((1, HEADS), F32), ((1, HEAD_DIM), F32), ((32, 32), F32), ((32, 32), F32), ((32, 32), F32),
        ((32, 8, 256), F32), ((1, C), F32), ((32, 8, 1024), F32), ((1, HIDDEN), F32), ((32, 4, 8, 256), F32),
    ]
    large = (0, 2, 3, 10, 12, 14)
    held = [
        ((N, C), BF16), ((N, C), F32), ((N, 1), F32), ((N, C), BF16), ((N, C), BF16), ((N, LANES), F32),
        ((N, LANES), BF16), ((N, LANES), F32), ((N, LANES), F32), ((N, LANES), F32),
        ((8, C), F32), ((8, 1), F32), ((N, C), BF16), ((N, HIDDEN), BF16), ((N, HIDDEN), BF16), ((N, HIDDEN), F32),
        ((N, C), BF16), ((N, C), F32), ((N, C), BF16), ((N, C), BF16), ((N, LANES), F32), ((N, C), BF16),
        ((N, C), BF16), ((N, LANES), BF16), ((N, LANES), BF16),
        ((C, 2 * LANES), BF16), ((C, 2 * LANES), BF16), ((256, 256), BF16), ((C, LANES), F32), ((C, LANES), BF16), ((C, LANES), BF16),
        ((C, LANES), BF16), ((C, LANES), BF16), ((1, LANES), F32), ((1, HIDDEN), F32), ((1, C), F32), ((1, C), F32), ((1, LANES), F32),
        ((C, LANES), F32), ((4, 128, 128), F32),
        *(((16, 16, 128), F32),) * 4, *(((16, 8, 128), F32),) * 4,
        *wide_buffers(WIDE_A, 16, 8, 1), *wide_buffers(WIDE_B, 8, 16, 2), *wide_buffers(TAIL, 16, 8, 1),
    ]
    sems = [pltpu.SemaphoreType.DMA((k, 16)) for k in (6, 6, 10, 10, 10)]
    sems += [pltpu.SemaphoreType.DMA((9,)), pltpu.VMEM((N, C), BF16)]
    anywhere = pl.BlockSpec(memory_space=pl.ANY)
    got = pl.pallas_call(
        kernel,
        out_shape=[jax.ShapeDtypeStruct(s, d) for s, d in outs],
        in_specs=[spec] * len(ins),
        out_specs=[anywhere if i in large else spec for i in range(len(outs))],
        scratch_shapes=[pltpu.VMEM(s, d) for s, d in held] + sems,
        compiler_params=pltpu.CompilerParams(
            collective_id=1, has_side_effects=True, vmem_limit_bytes=60 << 20
        ),
    )(*ins)
    got = pl.pallas_call(
        write_out,
        out_shape=[jax.ShapeDtypeStruct(s, d) for s, d in outs],
        in_specs=[spec] * len(outs),
        out_specs=[anywhere] * len(outs),
        scratch_shapes=[pltpu.SemaphoreType.DMA((len(outs),))],
    )(*got)
    shapes = (
        (N, C), (C,), (C, C), (C, C), (HEAD_DIM, SLICES), (HEADS,), (HEAD_DIM,), (32, 32), (32, 32), (32, 32), (C, C),
        (C,), (C, HIDDEN), (HIDDEN,), (HIDDEN, C),
    )
    return tuple(g.reshape(s) for g, s in zip(got, shapes))


def solution(mesh):
    rows, whole = P("pts", None), P()
    return jax.shard_map(
        per_device,
        mesh=mesh,
        in_specs=(rows, rows) + (whole,) * 14,
        out_specs=(rows,) + (whole,) * 14,
        check_vma=False,
    )
```

```python
import jax
import jax.numpy as jnp
from jax import lax
from jax.experimental import pallas as pl
from jax.experimental.pallas import tpu as pltpu
from jax.sharding import PartitionSpec as P

MESH = pl.DeviceIdType.MESH
F32 = jnp.float32
BF16 = jnp.bfloat16
C = 256
HEADS = 8
HEAD_DIM = 32
SLICES = 64
HIDDEN = 1024
LANES = HEADS * SLICES
N = 1024
TILE = 1024
PIECE = 1024
EPS = 1e-5
GELU_A = 0.7978845608028654
GELU_B = 0.044715

UP, DOWN_A, WIDE_A = 0, 1024, 1536
DOWN_B, OUT, WIDE_B = 0, 512, 768
GX, GFX, REST = 0, 256, 512
TAIL = 640


def nn(a, b):
    return lax.dot_general(a, b, (((1,), (0,)), ((), ())), preferred_element_type=F32)


def nt(a, b):
    return lax.dot_general(a, b, (((1,), (1,)), ((), ())), preferred_element_type=F32)


def tn(a, b):
    return lax.dot_general(a, b, (((0,), (0,)), ((), ())), preferred_element_type=F32)


def split(x):
    hi = x.astype(BF16)
    return hi, (x - hi.astype(F32)).astype(BF16)


def exact(dot, a, b):
    ah, al = split(a)
    bh, bl = split(b)
    return dot(ah, bh) + (dot(al, bh) + dot(ah, bl))


def remote(src, dst, send_sem, recv_sem, device):
    return pltpu.make_async_remote_copy(
        src_ref=src,
        dst_ref=dst,
        send_sem=send_sem,
        recv_sem=recv_sem,
        device_id=(device,),
        device_id_type=MESH,
    )


FAR_ZC = (8, 9, 7, 10, 6, 11, 5, 12, 4, 13, 3, 14, 2, 15, 1)
FAR_XY = (10, 9, 11, 6, 14, 8, 2, 5, 7, 13, 15, 1, 3, 4, 12)
FAR_Z = (4, 3, 5, 2, 6, 1, 7)


class Place:
    def __init__(self):
        me = lax.axis_index("pts")
        self.m, self.q = lax.rem(me, 16), lax.div(me, 16)
        self.core, self.z = lax.rem(self.m, 2), lax.div(self.m, 2)

    def zc(self, d):
        return lax.rem(self.m + d, 16)

    def xy(self, d):
        return lax.rem(self.q + d, 16)

    def zc_device(self, d):
        return self.q * 16 + self.zc(d)

    def xy_device(self, d):
        return self.xy(d) * 16 + self.m

    def z_device(self, d):
        return self.q * 16 + lax.rem(self.z + d, 8) * 2 + self.core

    def other_core(self):
        return self.q * 16 + self.z * 2 + (1 - self.core)


def greet(at):
    bar = pltpu.get_barrier_semaphore()
    for d in range(1, 16):
        pl.semaphore_signal(bar, inc=1, device_id=(at.zc_device(d),), device_id_type=MESH)
        pl.semaphore_signal(bar, inc=1, device_id=(at.xy_device(d),), device_id_type=MESH)


def greeted():
    pl.semaphore_wait(pltpu.get_barrier_semaphore(), 30)


class SmallSum:
    def __init__(self, at, x, got, plane, total, sems):
        self.at, self.x, self.got, self.plane, self.total, self.sems = at, x, got, plane, total, sems
        self.sent = []

    def _start(self, copies):
        for c in copies:
            c.start()
        self.phase = copies
        self.sent += copies

    def scatter(self):
        at, s = self.at, self.sems
        self._start(
            [remote(self.x.at[at.zc(d)], self.got.at[d], s.at[0, d], s.at[1, d], at.zc_device(d)) for d in FAR_ZC]
        )

    def middle(self):
        at, s = self.at, self.sems
        for c in self.phase:
            c.wait_recv()
        part = self.x[at.m]
        for d in range(1, 16):
            part = part + self.got[d]
        self.plane[at.q] = part
        mine = self.plane.at[at.q]
        self._start([remote(mine, mine, s.at[2, d], s.at[3, d], at.xy_device(d)) for d in FAR_XY])

    def gather(self):
        at, s = self.at, self.sems
        for c in self.phase:
            c.wait_recv()
        part = self.plane[0]
        for i in range(1, 16):
            part = part + self.plane[i]
        self.total[at.m] = part
        mine = self.total.at[at.m]
        self._start([remote(mine, mine, s.at[4, d], s.at[5, d], at.zc_device(d)) for d in FAR_ZC])

    def finish(self):
        for c in self.phase:
            c.wait_recv()
        for c in self.sent:
            c.wait_send()


class WideSum:
    def __init__(self, at, z_first, x, pair, got, column, total, sems):
        self.at, self.x, self.pair, self.got, self.column = at, x, pair, got, column
        self.total, self.sems = total, sems
        plane = (FAR_XY, at.q, at.xy, at.xy_device)
        line = (FAR_Z, at.z, lambda d: lax.rem(at.z + d, 8), at.z_device)
        self.first, self.second = (line, plane) if z_first else (plane, line)
        self.per = got.shape[1]
        self.sent = []

    def _slabs(self, index):
        return pl.ds(self.at.core * 16 + index * self.per, self.per)

    def _start(self, copies):
        for c in copies:
            c.start()
        self.phase = copies
        self.sent += copies

    def _arrive(self):
        for c in self.phase:
            c.wait_recv()

    def scatter_pair(self):
        at, s = self.at, self.sems
        there = pl.ds((1 - at.core) * 16, 16)
        self._start([remote(self.x.at[there], self.pair, s.at[0, 0], s.at[1, 0], at.other_core())])

    def scatter(self):
        s = self.sems
        self._arrive()
        base = self.at.core * 16

        def add(i, _):
            self.x[base + i] += self.pair[i]
            return 0

        lax.fori_loop(0, 16, add, 0)
        far, _, index, device = self.first
        self._start(
            [
                remote(self.x.at[self._slabs(index(d))], self.got.at[d], s.at[2, d], s.at[3, d], device(d))
                for d in far
            ]
        )

    def middle(self):
        s = self.sems
        self._arrive()
        mine = self.x[self._slabs(self.first[1])]
        for d in range(1, self.got.shape[0]):
            mine = mine + self.got[d]
        far, own, _, device = self.second
        self.column[own] = mine
        here = self.column.at[own]
        self._start([remote(here, here, s.at[4, d], s.at[5, d], device(d)) for d in far])

    def gather(self):
        s = self.sems
        self._arrive()
        mine = self.column[0]
        for i in range(1, self.column.shape[0]):
            mine = mine + self.column[i]
        far, own, _, device = self.first
        slabs = self._slabs(own)
        self.total[slabs] = mine
        here = self.total.at[slabs]
        self._start([remote(here, here, s.at[6, d], s.at[7, d], device(d)) for d in far])

    def gather_pair(self):
        at, s = self.at, self.sems
        far, own, _, _ = self.first
        count = len(far) + 1

        def forward(d):
            here = self.total.at[self._slabs(lax.rem(own + (count - d), count))]
            c = remote(here, here, s.at[8, d], s.at[9, d], at.other_core())
            c.start()
            return c

        passed = [forward(0)]
        for d, c in reversed(list(zip(far, self.phase))):
            c.wait_recv()
            passed.append(forward(d))
        self.phase = passed
        self.sent += passed

    def finish(self):
        self._arrive()
        for c in self.sent:
            c.wait_send()


def iota(shape, axis):
    return lax.broadcasted_iota(jnp.int32, shape, axis)


def head_mask(rows, per_row, columns, per_column):
    return iota((rows, columns), 0) // per_row == iota((rows, columns), 1) // per_column


def column_of(row):
    k = row.shape[1]
    eye = iota((k, k), 0) == iota((k, k), 1)
    return jnp.sum(jnp.where(eye, jnp.broadcast_to(row, (k, k)), 0.0), axis=1, keepdims=True)


def row_of(column):
    k = column.shape[0]
    eye = iota((k, k), 0) == iota((k, k), 1)
    return jnp.sum(jnp.where(eye, jnp.broadcast_to(column, (k, k)), 0.0), axis=0, keepdims=True)


def spread_heads(x):
    return jnp.where(head_mask(C, HEAD_DIM, LANES, SLICES), jnp.concatenate([x] * HEADS, axis=0), 0.0)


def fold_heads(x):
    x = jnp.where(head_mask(C, HEAD_DIM, LANES, SLICES), x, 0.0)
    return sum(x[h * HEAD_DIM : (h + 1) * HEAD_DIM] for h in range(HEADS))


def layer_norm(x):
    centered = x - jnp.mean(x, axis=-1, keepdims=True)
    inv = lax.rsqrt(jnp.mean(centered * centered, axis=-1, keepdims=True) + EPS)
    return centered * inv, inv


def layer_norm_back(d, hat, inv):
    a = jnp.mean(d, axis=-1, keepdims=True)
    b = jnp.mean(d * hat, axis=-1, keepdims=True)
    return inv * (d - a - hat * b)


def head_sums(x, ones):
    hi, lo = split(x)
    return jnp.concatenate(
        [nn(hi[:, k : k + 256], ones) + nn(lo[:, k : k + 256], ones) for k in (0, 256)], axis=1
    )


def kernel(
    points, cot, gain1, w_x, w_fx, w_slice, base, ada, wq, wk, wv, w_out, gain2, w_up, b_up, w_down,
    o_points, o_ggain1, o_gx, o_gfx, o_gslice, o_gbase, o_gada, o_gq, o_gk, o_gv, o_gout, o_ggain2, o_gup, o_gbup, o_gdown,
    nb, hat1, inv1, mid, feat, weight, weight_b, logits, rate, slope,
    hat2, inv2, n2b, act_b, dpre_b, dact, mixed_b, dfirst, dfirst_b, dmixed_b, dweight, dmid_b, dfeat_b, dlog_b, dtilt_b,
    ba_hi, ba_lo, ones, numer, so_b, so_l, dn_b, dn_l, denom_acc, bup_acc, gain2_acc, gain1_acc, base_acc, ada_acc, attn,
    s1_x, s1_got, s1_plane, s1_total, s2_x, s2_got, s2_plane, s2_total,
    a_x, a_pair, a_got, a_column, a_total,
    b_x, b_pair, b_got, b_column, b_total,
    tail_x, tail_pair, tail_got, tail_column, tail_total,
    s1_sems, s2_sems, a_sems, b_sems, tail_sems, out_sems, points_out, cot_t, nb_t, mid_t, wide_tile, half_tile,
):
    at = Place()
    greet(at)
    first_sum = SmallSum(at, s1_x, s1_got, s1_plane, s1_total, s1_sems)
    second_sum = SmallSum(at, s2_x, s2_got, s2_plane, s2_total, s2_sems)
    wide_a = WideSum(at, False, a_x, a_pair, a_got, a_column, a_total, a_sems)
    wide_b = WideSum(at, True, b_x, b_pair, b_got, b_column, b_total, b_sems)
    tail = WideSum(at, False, tail_x, tail_pair, tail_got, tail_column, tail_total, tail_sems)

    ws2 = jnp.concatenate([w_slice[...]] * 2, axis=1)
    hi, lo = split(spread_heads(jnp.concatenate([ws2] * 4, axis=1)))
    ba_hi[:, :LANES], ba_lo[:, :LANES] = hi, lo
    hi, lo = split(spread_heads(jnp.broadcast_to(column_of(ada[...]), (HEAD_DIM, LANES))))
    ba_hi[:, LANES:], ba_lo[:, LANES:] = hi, lo
    ones[...] = jnp.where(head_mask(256, SLICES, 256, SLICES), 1.0, 0.0).astype(BF16)
    base_row = jnp.sum(
        jnp.where(
            iota((HEADS, LANES), 0) == iota((HEADS, LANES), 1) // SLICES,
            jnp.broadcast_to(column_of(base[...]), (HEADS, LANES)),
            0.0,
        ),
        axis=0,
        keepdims=True,
    )
    inv_base = 1.0 / base_row

    numer[...] = jnp.zeros_like(numer)
    denom_acc[...] = jnp.zeros_like(denom_acc)

    def front(i, _):
        rows = pl.ds(pl.multiple_of(i * TILE, TILE), TILE)
        hat, inv = layer_norm(points[rows].astype(F32))
        hat1[rows] = hat
        inv1[rows] = inv
        normed = (hat * gain1[...]).astype(BF16)
        nb[rows] = normed
        md = nn(normed, w_x[...])
        ft = nn(normed, w_fx[...])
        mh, ml = split(md)
        mid[rows] = mh
        wide_tile[...] = nn(mh, ba_hi[...]) + (nn(ml, ba_hi[...]) + nn(mh, ba_lo[...]))

        def raise_piece(j, _):
            here = pl.ds(pl.multiple_of(j * PIECE, PIECE), PIECE)
            there = pl.ds(pl.multiple_of(i * TILE + j * PIECE, PIECE), PIECE)
            th = jnp.tanh(wide_tile[here, LANES:])
            rt = jnp.exp(-0.5 * th) * inv_base
            rate[there] = rt
            slope[there] = -0.5 * (1.0 - th * th)
            lg = wide_tile[here, :LANES] * rt
            logits[there] = lg
            half_tile[here] = jnp.exp(lg)
            return 0

        lax.fori_loop(0, TILE // PIECE, raise_piece, 0)
        raised = half_tile[...]
        w = raised / head_sums(raised, ones[...])
        weight[rows] = w
        denom_acc[...] += jnp.sum(w, axis=0, keepdims=True)
        wh, wl = split(w)
        weight_b[rows] = wh
        fh, fl = split(ft)
        feat[rows] = fh
        fht = fh.T
        numer[...] += nn(fht, wh) + (nn(fl.T, wh) + nn(fht, wl))
        return 0

    lax.fori_loop(0, N // TILE, front, 0)

    part = fold_heads(numer[...])
    for i in range(4):
        for j in range(4):
            s1_x[i * 4 + j, :8, :] = part[8 * i : 8 * i + 8, 128 * j : 128 * j + 128]
            s1_x[i * 4 + j, 8:, :] = denom_acc[:, 128 * j : 128 * j + 128]
    greeted()
    first_sum.scatter()

    def early(i, _):
        rows = pl.ds(pl.multiple_of(i * TILE, TILE), TILE)
        dact[rows] = nt(cot[rows], w_down[...])
        cot_t[:, rows] = cot[rows].T
        nb_t[:, rows] = nb[rows].T
        mid_t[:, rows] = mid[rows].T
        return 0

    lax.fori_loop(0, N // TILE, early, 0)
    first_sum.middle()
    first_sum.gather()
    first_sum.finish()

    numer_t = jnp.concatenate(
        [jnp.concatenate([s1_total[i * 4 + j, :8, :] for j in range(4)], axis=1) for i in range(4)], axis=0
    )
    denom = jnp.concatenate([s1_total[j, 8:9, :] for j in range(4)], axis=1) + EPS
    tok = numer_t / denom
    q_t = exact(tn, wq[...], tok)
    k_t = exact(tn, wk[...], tok)
    v_t = exact(tn, wv[...], tok)
    pair_mask = head_mask(128, SLICES, 128, SLICES)
    scale = HEAD_DIM ** (-0.5)
    outs = []
    for p in range(4):
        c = slice(128 * p, 128 * p + 128)
        e = jnp.where(pair_mask, jnp.exp(exact(tn, q_t[:, c], k_t[:, c]) * scale), 0.0)
        a = e / jnp.sum(e, axis=1, keepdims=True)
        attn[p] = a
        outs.append(exact(nt, v_t[:, c], a))
    so_b[...], so_l[...] = split(spread_heads(jnp.concatenate(outs, axis=1)))

    numer[...] = jnp.zeros_like(numer)
    bup_acc[...] = jnp.zeros_like(bup_acc)
    gain2_acc[...] = jnp.zeros_like(gain2_acc)

    def top(i, _):
        rows = pl.ds(pl.multiple_of(i * TILE, TILE), TILE)
        mb = (nt(weight_b[rows], so_b[...]) + nt(weight_b[rows], so_l[...])).astype(BF16)
        mixed_b[rows] = mb
        first = points[rows].astype(F32) + nn(mb, w_out[...])
        hat, inv = layer_norm(first)
        normed = (hat * gain2[...]).astype(BF16)
        n2b[rows] = normed
        wide_tile[...] = nn(normed, w_up[...])

        def gelu_piece(j, _):
            here = pl.ds(pl.multiple_of(j * PIECE, PIECE), PIECE)
            there = pl.ds(pl.multiple_of(i * TILE + j * PIECE, PIECE), PIECE)
            for k in range(0, HIDDEN, 256):
                lanes = slice(k, k + 256)
                x = wide_tile[here, lanes] + b_up[:, lanes]
                xx = x * x
                t = jnp.tanh(GELU_A * x * (1.0 + GELU_B * xx))
                half = 0.5 + 0.5 * t
                act_b[there, lanes] = (x * half).astype(BF16)
                grad = half + x * (0.5 * GELU_A - (0.5 * GELU_A) * (t * t)) * (1.0 + (3.0 * GELU_B) * xx)
                d = grad * dact[there, lanes]
                bup_acc[:, lanes] += jnp.sum(d, axis=0, keepdims=True)
                dpre_b[there, lanes] = d.astype(BF16)
            return 0

        lax.fori_loop(0, TILE // PIECE, gelu_piece, 0)
        dn = nt(dpre_b[rows, :], w_up[...])
        gain2_acc[...] += jnp.sum(dn * hat, axis=0, keepdims=True)
        df = cot[rows].astype(F32) + layer_norm_back(dn * gain2[...], hat, inv)
        dfirst[rows] = df
        dfb = df.astype(BF16)
        dfirst_b[rows] = dfb
        dm = nt(dfb, w_out[...])
        dmh, dml = split(dm)
        dmixed_b[rows] = dmh
        wh = weight_b[rows]
        numer[...] += tn(dmh, wh) + tn(dml, wh)
        return 0

    lax.fori_loop(0, N // TILE, top, 0)

    part = fold_heads(numer[...])
    for i in range(4):
        for j in range(4):
            s2_x[i * 4 + j] = part[8 * i : 8 * i + 8, 128 * j : 128 * j + 128]
    second_sum.scatter()

    n2b_t = n2b[...].T
    for k in range(0, HIDDEN, 256):
        a_x[:, :, UP + k : UP + k + 256] = nn(n2b_t, dpre_b[:, k : k + 256]).reshape(32, 8, 256)
    b_x[:, :, OUT : OUT + 256] = tn(mixed_b[...], dfirst_b[...]).reshape(32, 8, 256)
    second_sum.middle()
    for k in range(0, HIDDEN, 256):
        g = nn(cot_t[...], act_b[:, k : k + 256]).T.reshape(8, 4, 8, 256)
        for j in range(2):
            a_x[k // 32 : k // 32 + 8, :, DOWN_A + 256 * j : DOWN_A + 256 * j + 256] = g[:, j]
            b_x[k // 32 : k // 32 + 8, :, DOWN_B + 256 * j : DOWN_B + 256 * j + 256] = g[:, j + 2]
    wide_a.scatter_pair()
    wide_b.scatter_pair()

    def later(i, _):
        rows = pl.ds(pl.multiple_of(i * TILE, TILE), TILE)
        dweight[rows] = nn(dmixed_b[rows], so_b[...]) + nn(dmixed_b[rows], so_l[...])
        return 0

    second_sum.gather()
    wide_a.scatter()
    lax.fori_loop(0, N // TILE, later, 0)
    second_sum.finish()
    wide_b.scatter()

    dso = jnp.concatenate(
        [jnp.concatenate([s2_total[i * 4 + j] for j in range(4)], axis=1) for i in range(4)], axis=0
    )
    dq, dk, dv = [], [], []
    for p in range(4):
        c = slice(128 * p, 128 * p + 128)
        a = attn[p]
        dv.append(exact(nn, dso[:, c], a))
        da = exact(tn, dso[:, c], v_t[:, c])
        ds = a * (da - jnp.sum(a * da, axis=1, keepdims=True)) * scale
        dq.append(exact(nt, k_t[:, c], ds))
        dk.append(exact(nn, q_t[:, c], ds))
    dq, dk, dv = (jnp.concatenate(v, axis=1) for v in (dq, dk, dv))
    o_gq[...] = exact(nt, tok, dq)
    o_gk[...] = exact(nt, tok, dk)
    o_gv[...] = exact(nt, tok, dv)
    dtok = exact(nn, wq[...], dq) + exact(nn, wk[...], dk) + exact(nn, wv[...], dv)
    dnumer = dtok / denom
    ddenom = -jnp.sum(dnumer * tok, axis=0, keepdims=True)
    dn_b[...], dn_l[...] = split(spread_heads(dnumer))

    gain1_acc[...] = jnp.zeros_like(gain1_acc)
    base_acc[...] = jnp.zeros_like(base_acc)
    numer[...] = jnp.zeros_like(numer)
    ada_acc[...] = jnp.zeros_like(ada_acc)

    def lower(i, _):
        rows = pl.ds(pl.multiple_of(i * TILE, TILE), TILE)
        w = weight[rows]
        dw = dweight[rows] + (nn(feat[rows], dn_b[...]) + nn(feat[rows], dn_l[...])) + ddenom
        dl = w * (dw - head_sums(w * dw, ones[...]))
        g = dl * logits[rows]
        base_acc[...] += jnp.sum(g, axis=0, keepdims=True)
        dlb = (dl * rate[rows]).astype(BF16)
        gb = (g * slope[rows]).astype(BF16)
        dlog_b[rows] = dlb
        dtilt_b[rows] = gb
        dm = nt(dlb, ba_hi[:, :LANES]) + nt(gb, ba_hi[:, LANES:])
        dmb = dm.astype(BF16)
        dmid_b[rows] = dmb
        dfb = (nt(weight_b[rows], dn_b[...]) + nt(weight_b[rows], dn_l[...])).astype(BF16)
        dfeat_b[rows] = dfb
        mt = mid_t[:, rows]
        numer[...] += nn(mt, dlb)
        ada_acc[...] += nn(mt, gb)
        dn = nt(dmb, w_x[...]) + nt(dfb, w_fx[...])
        hat = hat1[rows]
        gain1_acc[...] += jnp.sum(dn * hat, axis=0, keepdims=True)
        points_out[rows] = (dfirst[rows] + layer_norm_back(dn * gain1[...], hat, inv1[rows])).astype(BF16)
        return 0

    lax.fori_loop(0, N // TILE, lower, 0)
    leaving = [pltpu.make_async_copy(points_out, o_points, out_sems.at[0])]
    leaving[0].start()
    wide_a.middle()
    wide_b.middle()
    tail_x[:, :, GX : GX + 256] = nn(nb_t[...], dmid_b[...]).reshape(32, 8, 256)
    tail_x[:, :, GFX : GFX + 256] = nn(nb_t[...], dfeat_b[...]).reshape(32, 8, 256)
    gs = fold_heads(numer[...])
    ga = fold_heads(ada_acc[...])
    gs = (gs[:, :128] + gs[:, 128:256]) + (gs[:, 256:384] + gs[:, 384:])
    ga = (ga[:, :128] + ga[:, 128:256]) + (ga[:, 256:384] + ga[:, 384:])
    rest = (REST, REST + 128)
    tail_x[:, :, REST : REST + 128] = jnp.zeros((32, 8, 128), F32)
    tail_x[0:4, :, REST : REST + 128] = gs.reshape(4, 8, 128)
    tail_x[4:8, :, REST : REST + 128] = ga.reshape(4, 8, 128)
    for i in range(8):
        tail_x[8, i : i + 1, rest[0] : rest[1]] = bup_acc[:, 128 * i : 128 * i + 128]
    for i in range(4):
        tail_x[9, i : i + 1, rest[0] : rest[1]] = base_acc[:, 128 * i : 128 * i + 128]
    for i in range(2):
        tail_x[10, i : i + 1, rest[0] : rest[1]] = gain1_acc[:, 128 * i : 128 * i + 128]
        tail_x[10, i + 2 : i + 3, rest[0] : rest[1]] = gain2_acc[:, 128 * i : 128 * i + 128]
    tail.scatter_pair()
    tail.scatter()
    wide_a.gather()
    wide_b.gather()
    tail.middle()
    tail.gather()
    wide_a.gather_pair()
    wide_b.gather_pair()
    tail.gather_pair()
    wide_a.finish()
    wide_b.finish()
    tail.finish()
    def leave(src, dst):
        c = pltpu.make_async_copy(src, dst, out_sems.at[len(leaving)])
        c.start()
        leaving.append(c)

    leave(a_total.at[:, :, UP : UP + 1024], o_gup)
    for j in range(2):
        leave(a_total.at[:, :, DOWN_A + 256 * j : DOWN_A + 256 * j + 256], o_gdown.at[:, j])
        leave(b_total.at[:, :, DOWN_B + 256 * j : DOWN_B + 256 * j + 256], o_gdown.at[:, j + 2])
    leave(b_total.at[:, :, OUT : OUT + 256], o_gout)
    leave(tail_total.at[:, :, GX : GX + 256], o_gx)
    leave(tail_total.at[:, :, GFX : GFX + 256], o_gfx)

    gs = tail_total[0:4, :, rest[0] : rest[1]].reshape(32, 128)
    o_gslice[...] = (gs + pltpu.roll(gs, SLICES, 1))[:, :SLICES]
    ga = tail_total[4:8, :, rest[0] : rest[1]].reshape(32, 128)
    o_gada[...] = row_of(jnp.sum(ga, axis=1, keepdims=True))
    gb = jnp.concatenate([tail_total[9, i : i + 1, rest[0] : rest[1]] for i in range(4)], axis=1)
    gb = gb * (-inv_base)
    pick = iota((HEADS, LANES), 0) == iota((HEADS, LANES), 1) // SLICES
    gb = jnp.sum(jnp.where(pick, jnp.broadcast_to(gb, (HEADS, LANES)), 0.0), axis=1, keepdims=True)
    o_gbase[...] = row_of(gb)
    for i in range(2):
        o_ggain1[:, 128 * i : 128 * i + 128] = tail_total[10, i : i + 1, rest[0] : rest[1]]
        o_ggain2[:, 128 * i : 128 * i + 128] = tail_total[10, i + 2 : i + 3, rest[0] : rest[1]]
    for i in range(8):
        o_gbup[:, 128 * i : 128 * i + 128] = tail_total[8, i : i + 1, rest[0] : rest[1]]
    for c in leaving:
        c.wait()


def write_out(*refs):
    count = len(refs) // 3
    sems = refs[-1]
    ins, outs, held = refs[:count], refs[count : 2 * count], refs[2 * count : 3 * count]
    arriving = [pltpu.make_async_copy(ins[i], held[i], sems.at[0, i]) for i in range(count)]
    leaving = [pltpu.make_async_copy(held[i], outs[i], sems.at[1, i]) for i in range(count)]
    for c in arriving:
        c.start()
    for a, c in zip(arriving, leaving):
        a.wait()
        c.start()
    for c in leaving:
        c.wait()


def wide_buffers(columns, first, second, per):
    return [
        (shape + (8, columns), F32) for shape in ((32,), (16,), (first, per), (second, per), (32,))
    ]


def per_device(*args):
    (points, cot, gain1, w_x, w_fx, w_slice, base, ada, wq, wk, wv, w_out, gain2, w_up, b_up, w_down) = args
    row = lambda v: v.reshape(1, -1)
    ins = (
        points, cot, row(gain1), w_x, w_fx, w_slice, row(base), row(ada), wq, wk, wv, w_out, row(gain2), w_up,
        row(b_up), w_down,
    )
    spec = pl.BlockSpec(memory_space=pltpu.VMEM)
    outs = [
        ((N, C), BF16), ((1, C), F32), ((32, 8, 256), F32), ((32, 8, 256), F32), ((HEAD_DIM, SLICES), F32),
        ((1, HEADS), F32), ((1, HEAD_DIM), F32), ((32, 32), F32), ((32, 32), F32), ((32, 32), F32),
        ((32, 8, 256), F32), ((1, C), F32), ((32, 8, 1024), F32), ((1, HIDDEN), F32), ((32, 4, 8, 256), F32),
    ]
    large = (0, 2, 3, 10, 12, 14)
    held = [
        ((N, C), BF16), ((N, C), F32), ((N, 1), F32), ((N, C), BF16), ((N, C), BF16), ((N, LANES), F32),
        ((N, LANES), BF16), ((N, LANES), F32), ((N, LANES), F32), ((N, LANES), F32),
        ((8, C), F32), ((8, 1), F32), ((N, C), BF16), ((N, HIDDEN), BF16), ((N, HIDDEN), BF16), ((N, HIDDEN), F32),
        ((N, C), BF16), ((N, C), F32), ((N, C), BF16), ((N, C), BF16), ((N, LANES), F32), ((N, C), BF16),
        ((N, C), BF16), ((N, LANES), BF16), ((N, LANES), BF16),
        ((C, 2 * LANES), BF16), ((C, 2 * LANES), BF16), ((256, 256), BF16), ((C, LANES), F32), ((C, LANES), BF16), ((C, LANES), BF16),
        ((C, LANES), BF16), ((C, LANES), BF16), ((1, LANES), F32), ((1, HIDDEN), F32), ((1, C), F32), ((1, C), F32), ((1, LANES), F32),
        ((C, LANES), F32), ((4, 128, 128), F32),
        *(((16, 9, 128), F32),) * 4, *(((16, 8, 128), F32),) * 4,
        *wide_buffers(WIDE_A, 16, 8, 1), *wide_buffers(WIDE_B, 8, 16, 2), *wide_buffers(TAIL, 16, 8, 1),
    ]
    sems = [pltpu.SemaphoreType.DMA((k, 16)) for k in (6, 6, 10, 10, 10)]
    sems += [pltpu.SemaphoreType.DMA((9,)), pltpu.VMEM((N, C), BF16)]
    sems += [pltpu.VMEM((C, N), BF16)] * 3 + [pltpu.VMEM((TILE, HIDDEN), F32), pltpu.VMEM((TILE, LANES), F32)]
    anywhere = pl.BlockSpec(memory_space=pl.ANY)
    got = pl.pallas_call(
        kernel,
        out_shape=[jax.ShapeDtypeStruct(s, d) for s, d in outs],
        in_specs=[spec] * len(ins),
        out_specs=[anywhere if i in large else spec for i in range(len(outs))],
        scratch_shapes=[pltpu.VMEM(s, d) for s, d in held] + sems,
        compiler_params=pltpu.CompilerParams(
            collective_id=1, has_side_effects=True, vmem_limit_bytes=60 << 20
        ),
    )(*ins)
    got = pl.pallas_call(
        write_out,
        out_shape=[jax.ShapeDtypeStruct(s, d) for s, d in outs],
        in_specs=[anywhere] * len(outs),
        out_specs=[anywhere] * len(outs),
        scratch_shapes=[pltpu.VMEM(s, d) for s, d in outs] + [pltpu.SemaphoreType.DMA((2, len(outs)))],
    )(*got)
    shapes = (
        (N, C), (C,), (C, C), (C, C), (HEAD_DIM, SLICES), (HEADS,), (HEAD_DIM,), (32, 32), (32, 32), (32, 32), (C, C),
        (C,), (C, HIDDEN), (HIDDEN,), (HIDDEN, C),
    )
    return tuple(g.reshape(s) for g, s in zip(got, shapes))


def solution(mesh):
    rows, whole = P("pts", None), P()
    return jax.shard_map(
        per_device,
        mesh=mesh,
        in_specs=(rows, rows) + (whole,) * 14,
        out_specs=(rows,) + (whole,) * 14,
        check_vma=False,
    )
```

```python
import jax
import jax.numpy as jnp
from jax import lax
from jax.experimental import pallas as pl
from jax.experimental.pallas import tpu as pltpu
from jax.sharding import PartitionSpec as P

MESH = pl.DeviceIdType.MESH
F32 = jnp.float32
BF16 = jnp.bfloat16
C = 256
HEADS = 8
HEAD_DIM = 32
SLICES = 64
HIDDEN = 1024
LANES = HEADS * SLICES
N = 1024
TILE = 1024
PIECE = 1024
EPS = 1e-5
GELU_A = 0.7978845608028654
GELU_B = 0.044715

GX, GFX, OUT, REST = 0, 256, 512, 768
TAIL = 896


def nn(a, b):
    return lax.dot_general(a, b, (((1,), (0,)), ((), ())), preferred_element_type=F32)


def nt(a, b):
    return lax.dot_general(a, b, (((1,), (1,)), ((), ())), preferred_element_type=F32)


def tn(a, b):
    return lax.dot_general(a, b, (((0,), (0,)), ((), ())), preferred_element_type=F32)


def split(x):
    hi = x.astype(BF16)
    return hi, (x - hi.astype(F32)).astype(BF16)


def exact(dot, a, b):
    ah, al = split(a)
    bh, bl = split(b)
    return dot(ah, bh) + (dot(al, bh) + dot(ah, bl))


def remote(src, dst, send_sem, recv_sem, device):
    return pltpu.make_async_remote_copy(
        src_ref=src,
        dst_ref=dst,
        send_sem=send_sem,
        recv_sem=recv_sem,
        device_id=(device,),
        device_id_type=MESH,
    )


FAR_ZC = (8, 9, 7, 10, 6, 11, 5, 12, 4, 13, 3, 14, 2, 15, 1)
FAR_XY = (10, 9, 11, 6, 14, 8, 2, 5, 7, 13, 15, 1, 3, 4, 12)
FAR_Z = (4, 3, 5, 2, 6, 1, 7)


class Place:
    def __init__(self):
        me = lax.axis_index("pts")
        self.m, self.q = lax.rem(me, 16), lax.div(me, 16)
        self.core, self.z = lax.rem(self.m, 2), lax.div(self.m, 2)
        self.x, self.y = lax.div(self.q, 4), lax.rem(self.q, 4)

    def zc(self, d):
        return lax.rem(self.m + d, 16)

    def xy(self, d):
        return lax.rem(self.q + d, 16)

    def zc_device(self, d):
        return self.q * 16 + self.zc(d)

    def xy_device(self, d):
        return self.xy(d) * 16 + self.m

    def along_x(self, d):
        return lax.rem(self.x + d, 4)

    def along_y(self, d):
        return lax.rem(self.y + d, 4)

    def x_device(self, d):
        return (self.along_x(d) * 4 + self.y) * 16 + self.m

    def y_device(self, d):
        return (self.x * 4 + self.along_y(d)) * 16 + self.m

    def z_device(self, d):
        return self.q * 16 + lax.rem(self.z + d, 8) * 2 + self.core

    def other_core(self):
        return self.q * 16 + self.z * 2 + (1 - self.core)


def greet(at):
    bar = pltpu.get_barrier_semaphore()
    for d in range(1, 16):
        pl.semaphore_signal(bar, inc=1, device_id=(at.zc_device(d),), device_id_type=MESH)
        pl.semaphore_signal(bar, inc=1, device_id=(at.xy_device(d),), device_id_type=MESH)


def greeted():
    pl.semaphore_wait(pltpu.get_barrier_semaphore(), 30)


class SmallSum:
    def __init__(self, at, x, got, plane, total, sems):
        self.at, self.x, self.got, self.plane, self.total, self.sems = at, x, got, plane, total, sems
        self.sent = []

    def _start(self, copies):
        for c in copies:
            c.start()
        self.phase = copies
        self.sent += copies

    def scatter(self):
        at, s = self.at, self.sems
        self._start(
            [remote(self.x.at[at.zc(d)], self.got.at[d], s.at[0, d], s.at[1, d], at.zc_device(d)) for d in FAR_ZC]
        )

    def middle(self):
        at, s = self.at, self.sems
        for c in self.phase:
            c.wait_recv()
        part = self.x[at.m]
        for d in range(1, 16):
            part = part + self.got[d]
        self.plane[at.q] = part
        mine = self.plane.at[at.q]
        self._start([remote(mine, mine, s.at[2, d], s.at[3, d], at.xy_device(d)) for d in FAR_XY])

    def gather(self):
        at, s = self.at, self.sems
        for c in self.phase:
            c.wait_recv()
        part = self.plane[0]
        for i in range(1, 16):
            part = part + self.plane[i]
        self.total[at.m] = part
        mine = self.total.at[at.m]
        self._start([remote(mine, mine, s.at[4, d], s.at[5, d], at.zc_device(d)) for d in FAR_ZC])

    def finish(self):
        for c in self.phase:
            c.wait_recv()
        for c in self.sent:
            c.wait_send()


class WideSum:
    def __init__(self, at, z_first, x, pair, got, column, total, sems):
        self.at, self.x, self.pair, self.got, self.column = at, x, pair, got, column
        self.total, self.sems = total, sems
        plane = (FAR_XY, at.q, at.xy, at.xy_device)
        line = (FAR_Z, at.z, lambda d: lax.rem(at.z + d, 8), at.z_device)
        self.first, self.second = (line, plane) if z_first else (plane, line)
        self.per = got.shape[1]
        self.sent = []

    def _slabs(self, index):
        return pl.ds(self.at.core * 16 + index * self.per, self.per)

    def _start(self, copies):
        for c in copies:
            c.start()
        self.phase = copies
        self.sent += copies

    def _arrive(self):
        for c in self.phase:
            c.wait_recv()

    def scatter_pair(self):
        at, s = self.at, self.sems
        there = pl.ds((1 - at.core) * 16, 16)
        self._start([remote(self.x.at[there], self.pair, s.at[0, 0], s.at[1, 0], at.other_core())])

    def scatter(self):
        s = self.sems
        self._arrive()
        base = self.at.core * 16

        def add(i, _):
            self.x[base + i] += self.pair[i]
            return 0

        lax.fori_loop(0, 16, add, 0)
        far, _, index, device = self.first
        self._start(
            [
                remote(self.x.at[self._slabs(index(d))], self.got.at[d], s.at[2, d], s.at[3, d], device(d))
                for d in far
            ]
        )

    def middle(self):
        s = self.sems
        self._arrive()
        mine = self.x[self._slabs(self.first[1])]
        for d in range(1, self.got.shape[0]):
            mine = mine + self.got[d]
        far, own, _, device = self.second
        self.column[own] = mine
        here = self.column.at[own]
        self._start([remote(here, here, s.at[4, d], s.at[5, d], device(d)) for d in far])

    def gather(self):
        s = self.sems
        self._arrive()
        mine = self.column[0]
        for i in range(1, self.column.shape[0]):
            mine = mine + self.column[i]
        far, own, _, device = self.first
        slabs = self._slabs(own)
        self.total[slabs] = mine
        here = self.total.at[slabs]
        self._start([remote(here, here, s.at[6, d], s.at[7, d], device(d)) for d in far])

    def gather_pair(self):
        at, s = self.at, self.sems
        far, own, _, _ = self.first
        count = len(far) + 1

        def forward(d):
            here = self.total.at[self._slabs(lax.rem(own + (count - d), count))]
            c = remote(here, here, s.at[8, d], s.at[9, d], at.other_core())
            c.start()
            return c

        passed = [forward(0)]
        for d, c in reversed(list(zip(far, self.phase))):
            c.wait_recv()
            passed.append(forward(d))
        self.phase = passed
        self.sent += passed

    def finish(self):
        self._arrive()
        for c in self.sent:
            c.wait_send()


class DeepSum:
    def __init__(self, at, y_first, x, pair, got, got2, line, line_got, line_sum, total, sems):
        self.at, self.x, self.pair, self.got, self.got2 = at, x, pair, got, got2
        self.line, self.line_got, self.line_sum = line, line_got, line_sum
        self.total, self.sems = total, sems
        along_x = (at.x, at.along_x, at.x_device)
        along_y = (at.y, at.along_y, at.y_device)
        self.first, self.second = (along_y, along_x) if y_first else (along_x, along_y)
        self.base = at.core * 16
        self.slab = self.base + 4 * self.first[0] + self.second[0]
        self.sent = []

    def _chunk(self, index):
        return pl.ds(self.base + 4 * index, 4)

    def _start(self, step, moves):
        s = self.sems
        copies = [remote(src, dst, s.at[2 * step, d], s.at[2 * step + 1, d], device) for d, src, dst, device in moves]
        for c in copies:
            c.start()
        self.phase = copies
        self.sent += copies

    def _arrive(self):
        for c in self.phase:
            c.wait_recv()

    def scatter_pair(self):
        there = pl.ds((1 - self.at.core) * 16, 16)
        self._start(0, [(0, self.x.at[there], self.pair, self.at.other_core())])

    def scatter(self):
        self._arrive()

        def add(i, _):
            self.x[self.base + i] += self.pair[i]
            return 0

        lax.fori_loop(0, 16, add, 0)
        _, index, device = self.first
        self._start(1, [(d, self.x.at[self._chunk(index(d))], self.got.at[d], device(d)) for d in (2, 1, 3)])

    def scatter_second(self):
        self._arrive()
        own = self.base + 4 * self.first[0]

        def add(i, _):
            self.x[own + i] += self.got[1, i] + (self.got[2, i] + self.got[3, i])
            return 0

        lax.fori_loop(0, 4, add, 0)
        _, index, device = self.second
        self._start(2, [(d, self.x.at[own + index(d)], self.got2.at[d], device(d)) for d in (2, 1, 3)])

    def scatter_line(self):
        self._arrive()
        mine = self.x[self.slab] + self.got2[1] + (self.got2[2] + self.got2[3])
        for i in range(8):
            self.line[i] = mine[:, 128 * i : 128 * i + 128]
        at = self.at
        self._start(
            3, [(d, self.line.at[lax.rem(at.z + d, 8)], self.line_got.at[d], at.z_device(d)) for d in FAR_Z]
        )

    def gather_line(self):
        self._arrive()
        at = self.at
        part = self.line[at.z]
        for d in range(1, 8):
            part = part + self.line_got[d]
        self.line_sum[at.z] = part
        here = self.line_sum.at[at.z]
        self._start(4, [(d, here, here, at.z_device(d)) for d in FAR_Z])

    def gather_second(self):
        self._arrive()
        self.total[self.slab] = jnp.concatenate([self.line_sum[i] for i in range(8)], axis=1)
        here = self.total.at[self.slab]
        _, _, device = self.second
        self._start(5, [(d, here, here, device(d)) for d in (2, 1, 3)])

    def gather(self):
        self._arrive()
        own, _, device = self.first
        here = self.total.at[self._chunk(own)]
        self._start(6, [(d, here, here, device(d)) for d in (2, 1, 3)])

    def gather_pair(self):
        own, _, _ = self.first
        arriving, passed = self.phase, []
        for d, c in ((0, None), (1, arriving[1]), (3, arriving[2]), (2, arriving[0])):
            if c is not None:
                c.wait_recv()
            here = self.total.at[self._chunk(lax.rem(own + (4 - d), 4))]
            self._start(7, [(d, here, here, self.at.other_core())])
            passed += self.phase
        self.phase = passed

    def finish(self):
        self._arrive()
        for c in self.sent:
            c.wait_send()


def iota(shape, axis):
    return lax.broadcasted_iota(jnp.int32, shape, axis)


def head_mask(rows, per_row, columns, per_column):
    return iota((rows, columns), 0) // per_row == iota((rows, columns), 1) // per_column


def column_of(row):
    k = row.shape[1]
    eye = iota((k, k), 0) == iota((k, k), 1)
    return jnp.sum(jnp.where(eye, jnp.broadcast_to(row, (k, k)), 0.0), axis=1, keepdims=True)


def row_of(column):
    k = column.shape[0]
    eye = iota((k, k), 0) == iota((k, k), 1)
    return jnp.sum(jnp.where(eye, jnp.broadcast_to(column, (k, k)), 0.0), axis=0, keepdims=True)


def spread_heads(x):
    return jnp.where(head_mask(C, HEAD_DIM, LANES, SLICES), jnp.concatenate([x] * HEADS, axis=0), 0.0)


def fold_heads(x):
    x = jnp.where(head_mask(C, HEAD_DIM, LANES, SLICES), x, 0.0)
    return sum(x[h * HEAD_DIM : (h + 1) * HEAD_DIM] for h in range(HEADS))


def layer_norm(x):
    centered = x - jnp.mean(x, axis=-1, keepdims=True)
    inv = lax.rsqrt(jnp.mean(centered * centered, axis=-1, keepdims=True) + EPS)
    return centered * inv, inv


def layer_norm_back(d, hat, inv):
    a = jnp.mean(d, axis=-1, keepdims=True)
    b = jnp.mean(d * hat, axis=-1, keepdims=True)
    return inv * (d - a - hat * b)


def head_sums(x, ones):
    hi, lo = split(x)
    return jnp.concatenate(
        [nn(hi[:, k : k + 256], ones) + nn(lo[:, k : k + 256], ones) for k in (0, 256)], axis=1
    )


def kernel(
    points, cot, gain1, w_x, w_fx, w_slice, base, ada, wq, wk, wv, w_out, gain2, w_up, b_up, w_down,
    o_points, o_ggain1, o_gx, o_gfx, o_gslice, o_gbase, o_gada, o_gq, o_gk, o_gv, o_gout, o_ggain2, o_gup, o_gbup, o_gdown,
    nb, hat1, inv1, mid, feat, weight, weight_b, logits, rate, slope,
    hat2, inv2, n2b, act_b, dpre_b, dact, mixed_b, dfirst, dfirst_b, dmixed_b, dweight, dmid_b, dfeat_b, dlog_b, dtilt_b,
    ba_hi, ba_lo, ones, numer, so_b, so_l, dn_b, dn_l, denom_acc, bup_acc, gain2_acc, gain1_acc, base_acc, ada_acc, attn,
    s1_x, s1_got, s1_plane, s1_total, s2_x, s2_got, s2_plane, s2_total,
    up_x, up_pair, up_got, up_got2, up_line, up_line_got, up_line_sum, up_total,
    down_x, down_pair, down_got, down_got2, down_line, down_line_got, down_line_sum, down_total,
    tail_x, tail_pair, tail_got, tail_column, tail_total,
    s1_sems, s2_sems, up_sems, down_sems, tail_sems, out_sems, points_out, cot_t, nb_t, mid_t, wide_tile, half_tile,
):
    at = Place()
    greet(at)
    first_sum = SmallSum(at, s1_x, s1_got, s1_plane, s1_total, s1_sems)
    second_sum = SmallSum(at, s2_x, s2_got, s2_plane, s2_total, s2_sems)
    up = DeepSum(at, False, up_x, up_pair, up_got, up_got2, up_line, up_line_got, up_line_sum, up_total, up_sems)
    down = DeepSum(
        at, True, down_x, down_pair, down_got, down_got2, down_line, down_line_got, down_line_sum, down_total, down_sems
    )
    tail = WideSum(at, False, tail_x, tail_pair, tail_got, tail_column, tail_total, tail_sems)

    ws2 = jnp.concatenate([w_slice[...]] * 2, axis=1)
    hi, lo = split(spread_heads(jnp.concatenate([ws2] * 4, axis=1)))
    ba_hi[:, :LANES], ba_lo[:, :LANES] = hi, lo
    hi, lo = split(spread_heads(jnp.broadcast_to(column_of(ada[...]), (HEAD_DIM, LANES))))
    ba_hi[:, LANES:], ba_lo[:, LANES:] = hi, lo
    ones[...] = jnp.where(head_mask(256, SLICES, 256, SLICES), 1.0, 0.0).astype(BF16)
    base_row = jnp.sum(
        jnp.where(
            iota((HEADS, LANES), 0) == iota((HEADS, LANES), 1) // SLICES,
            jnp.broadcast_to(column_of(base[...]), (HEADS, LANES)),
            0.0,
        ),
        axis=0,
        keepdims=True,
    )
    inv_base = 1.0 / base_row

    numer[...] = jnp.zeros_like(numer)
    denom_acc[...] = jnp.zeros_like(denom_acc)

    def front(i, _):
        rows = pl.ds(pl.multiple_of(i * TILE, TILE), TILE)
        hat, inv = layer_norm(points[rows].astype(F32))
        hat1[rows] = hat
        inv1[rows] = inv
        normed = (hat * gain1[...]).astype(BF16)
        nb[rows] = normed
        md = nn(normed, w_x[...])
        ft = nn(normed, w_fx[...])
        mh, ml = split(md)
        mid[rows] = mh
        wide_tile[...] = nn(mh, ba_hi[...]) + (nn(ml, ba_hi[...]) + nn(mh, ba_lo[...]))

        def raise_piece(j, _):
            here = pl.ds(pl.multiple_of(j * PIECE, PIECE), PIECE)
            there = pl.ds(pl.multiple_of(i * TILE + j * PIECE, PIECE), PIECE)
            th = jnp.tanh(wide_tile[here, LANES:])
            rt = jnp.exp(-0.5 * th) * inv_base
            rate[there] = rt
            slope[there] = -0.5 * (1.0 - th * th)
            lg = wide_tile[here, :LANES] * rt
            logits[there] = lg
            half_tile[here] = jnp.exp(lg)
            return 0

        lax.fori_loop(0, TILE // PIECE, raise_piece, 0)
        raised = half_tile[...]
        w = raised / head_sums(raised, ones[...])
        weight[rows] = w
        denom_acc[...] += jnp.sum(w, axis=0, keepdims=True)
        wh, wl = split(w)
        weight_b[rows] = wh
        fh, fl = split(ft)
        feat[rows] = fh
        fht = fh.T
        numer[...] += nn(fht, wh) + (nn(fl.T, wh) + nn(fht, wl))
        return 0

    lax.fori_loop(0, N // TILE, front, 0)

    part = fold_heads(numer[...])
    for i in range(4):
        for j in range(4):
            s1_x[i * 4 + j, :8, :] = part[8 * i : 8 * i + 8, 128 * j : 128 * j + 128]
            s1_x[i * 4 + j, 8:, :] = denom_acc[:, 128 * j : 128 * j + 128]
    greeted()
    first_sum.scatter()

    def early(i, _):
        rows = pl.ds(pl.multiple_of(i * TILE, TILE), TILE)
        dact[rows] = nt(cot[rows], w_down[...])
        cot_t[:, rows] = cot[rows].T
        nb_t[:, rows] = nb[rows].T
        mid_t[:, rows] = mid[rows].T
        return 0

    lax.fori_loop(0, N // TILE, early, 0)
    first_sum.middle()
    first_sum.gather()
    first_sum.finish()

    numer_t = jnp.concatenate(
        [jnp.concatenate([s1_total[i * 4 + j, :8, :] for j in range(4)], axis=1) for i in range(4)], axis=0
    )
    denom = jnp.concatenate([s1_total[j, 8:9, :] for j in range(4)], axis=1) + EPS
    tok = numer_t / denom
    q_t = exact(tn, wq[...], tok)
    k_t = exact(tn, wk[...], tok)
    v_t = exact(tn, wv[...], tok)
    pair_mask = head_mask(128, SLICES, 128, SLICES)
    scale = HEAD_DIM ** (-0.5)
    outs = []
    for p in range(4):
        c = slice(128 * p, 128 * p + 128)
        e = jnp.where(pair_mask, jnp.exp(exact(tn, q_t[:, c], k_t[:, c]) * scale), 0.0)
        a = e / jnp.sum(e, axis=1, keepdims=True)
        attn[p] = a
        outs.append(exact(nt, v_t[:, c], a))
    so_b[...], so_l[...] = split(spread_heads(jnp.concatenate(outs, axis=1)))

    numer[...] = jnp.zeros_like(numer)
    bup_acc[...] = jnp.zeros_like(bup_acc)
    gain2_acc[...] = jnp.zeros_like(gain2_acc)

    def top(i, _):
        rows = pl.ds(pl.multiple_of(i * TILE, TILE), TILE)
        mb = (nt(weight_b[rows], so_b[...]) + nt(weight_b[rows], so_l[...])).astype(BF16)
        mixed_b[rows] = mb
        first = points[rows].astype(F32) + nn(mb, w_out[...])
        hat, inv = layer_norm(first)
        normed = (hat * gain2[...]).astype(BF16)
        n2b[rows] = normed
        wide_tile[...] = nn(normed, w_up[...])

        def gelu_piece(j, _):
            here = pl.ds(pl.multiple_of(j * PIECE, PIECE), PIECE)
            there = pl.ds(pl.multiple_of(i * TILE + j * PIECE, PIECE), PIECE)
            for k in range(0, HIDDEN, 256):
                lanes = slice(k, k + 256)
                x = wide_tile[here, lanes] + b_up[:, lanes]
                xx = x * x
                t = jnp.tanh(GELU_A * x * (1.0 + GELU_B * xx))
                half = 0.5 + 0.5 * t
                act_b[there, lanes] = (x * half).astype(BF16)
                grad = half + x * (0.5 * GELU_A - (0.5 * GELU_A) * (t * t)) * (1.0 + (3.0 * GELU_B) * xx)
                d = grad * dact[there, lanes]
                bup_acc[:, lanes] += jnp.sum(d, axis=0, keepdims=True)
                dpre_b[there, lanes] = d.astype(BF16)
            return 0

        lax.fori_loop(0, TILE // PIECE, gelu_piece, 0)
        dn = nt(dpre_b[rows, :], w_up[...])
        gain2_acc[...] += jnp.sum(dn * hat, axis=0, keepdims=True)
        df = cot[rows].astype(F32) + layer_norm_back(dn * gain2[...], hat, inv)
        dfirst[rows] = df
        dfb = df.astype(BF16)
        dfirst_b[rows] = dfb
        dm = nt(dfb, w_out[...])
        dmh, dml = split(dm)
        dmixed_b[rows] = dmh
        wh = weight_b[rows]
        numer[...] += tn(dmh, wh) + tn(dml, wh)
        return 0

    lax.fori_loop(0, N // TILE, top, 0)

    part = fold_heads(numer[...])
    for i in range(4):
        for j in range(4):
            s2_x[i * 4 + j] = part[8 * i : 8 * i + 8, 128 * j : 128 * j + 128]
    second_sum.scatter()

    n2b_t = n2b[...].T
    for k in range(0, HIDDEN, 256):
        up_x[:, :, k : k + 256] = nn(n2b_t, dpre_b[:, k : k + 256]).reshape(32, 8, 256)
    second_sum.middle()
    for k in range(0, HIDDEN, 256):
        g = nn(cot_t[...], act_b[:, k : k + 256]).T.reshape(8, 4, 8, 256)
        for j in range(4):
            down_x[k // 32 : k // 32 + 8, :, 256 * j : 256 * j + 256] = g[:, j]
    up.scatter_pair()
    down.scatter_pair()

    def later(i, _):
        rows = pl.ds(pl.multiple_of(i * TILE, TILE), TILE)
        dweight[rows] = nn(dmixed_b[rows], so_b[...]) + nn(dmixed_b[rows], so_l[...])
        return 0

    second_sum.gather()
    up.scatter()
    down.scatter()
    lax.fori_loop(0, N // TILE, later, 0)
    tail_x[:, :, OUT : OUT + 256] = tn(mixed_b[...], dfirst_b[...]).reshape(32, 8, 256)
    second_sum.finish()

    dso = jnp.concatenate(
        [jnp.concatenate([s2_total[i * 4 + j] for j in range(4)], axis=1) for i in range(4)], axis=0
    )
    dq, dk, dv = [], [], []
    for p in range(4):
        c = slice(128 * p, 128 * p + 128)
        a = attn[p]
        dv.append(exact(nn, dso[:, c], a))
        da = exact(tn, dso[:, c], v_t[:, c])
        ds = a * (da - jnp.sum(a * da, axis=1, keepdims=True)) * scale
        dq.append(exact(nt, k_t[:, c], ds))
        dk.append(exact(nn, q_t[:, c], ds))
    dq, dk, dv = (jnp.concatenate(v, axis=1) for v in (dq, dk, dv))
    o_gq[...] = exact(nt, tok, dq)
    o_gk[...] = exact(nt, tok, dk)
    o_gv[...] = exact(nt, tok, dv)
    dtok = exact(nn, wq[...], dq) + exact(nn, wk[...], dk) + exact(nn, wv[...], dv)
    dnumer = dtok / denom
    ddenom = -jnp.sum(dnumer * tok, axis=0, keepdims=True)
    dn_b[...], dn_l[...] = split(spread_heads(dnumer))

    gain1_acc[...] = jnp.zeros_like(gain1_acc)
    base_acc[...] = jnp.zeros_like(base_acc)
    numer[...] = jnp.zeros_like(numer)
    ada_acc[...] = jnp.zeros_like(ada_acc)

    def lower(i, _):
        rows = pl.ds(pl.multiple_of(i * TILE, TILE), TILE)
        w = weight[rows]
        dw = dweight[rows] + (nn(feat[rows], dn_b[...]) + nn(feat[rows], dn_l[...])) + ddenom
        dl = w * (dw - head_sums(w * dw, ones[...]))
        g = dl * logits[rows]
        base_acc[...] += jnp.sum(g, axis=0, keepdims=True)
        dlb = (dl * rate[rows]).astype(BF16)
        gb = (g * slope[rows]).astype(BF16)
        dlog_b[rows] = dlb
        dtilt_b[rows] = gb
        dm = nt(dlb, ba_hi[:, :LANES]) + nt(gb, ba_hi[:, LANES:])
        dmb = dm.astype(BF16)
        dmid_b[rows] = dmb
        dfb = (nt(weight_b[rows], dn_b[...]) + nt(weight_b[rows], dn_l[...])).astype(BF16)
        dfeat_b[rows] = dfb
        mt = mid_t[:, rows]
        numer[...] += nn(mt, dlb)
        ada_acc[...] += nn(mt, gb)
        dn = nt(dmb, w_x[...]) + nt(dfb, w_fx[...])
        hat = hat1[rows]
        gain1_acc[...] += jnp.sum(dn * hat, axis=0, keepdims=True)
        points_out[rows] = (dfirst[rows] + layer_norm_back(dn * gain1[...], hat, inv1[rows])).astype(BF16)
        return 0

    up.scatter_second()
    down.scatter_second()
    lax.fori_loop(0, N // TILE, lower, 0)
    leaving = [pltpu.make_async_copy(points_out, o_points, out_sems.at[0])]
    leaving[0].start()
    up.scatter_line()
    down.scatter_line()
    tail_x[:, :, GX : GX + 256] = nn(nb_t[...], dmid_b[...]).reshape(32, 8, 256)
    tail_x[:, :, GFX : GFX + 256] = nn(nb_t[...], dfeat_b[...]).reshape(32, 8, 256)
    gs = fold_heads(numer[...])
    ga = fold_heads(ada_acc[...])
    gs = (gs[:, :128] + gs[:, 128:256]) + (gs[:, 256:384] + gs[:, 384:])
    ga = (ga[:, :128] + ga[:, 128:256]) + (ga[:, 256:384] + ga[:, 384:])
    rest = (REST, REST + 128)
    tail_x[:, :, REST : REST + 128] = jnp.zeros((32, 8, 128), F32)
    tail_x[0:4, :, REST : REST + 128] = gs.reshape(4, 8, 128)
    tail_x[4:8, :, REST : REST + 128] = ga.reshape(4, 8, 128)
    for i in range(8):
        tail_x[8, i : i + 1, rest[0] : rest[1]] = bup_acc[:, 128 * i : 128 * i + 128]
    for i in range(4):
        tail_x[9, i : i + 1, rest[0] : rest[1]] = base_acc[:, 128 * i : 128 * i + 128]
    for i in range(2):
        tail_x[10, i : i + 1, rest[0] : rest[1]] = gain1_acc[:, 128 * i : 128 * i + 128]
        tail_x[10, i + 2 : i + 3, rest[0] : rest[1]] = gain2_acc[:, 128 * i : 128 * i + 128]
    def leave(src, dst):
        c = pltpu.make_async_copy(src, dst, out_sems.at[len(leaving)])
        c.start()
        leaving.append(c)

    tail.scatter_pair()
    up.gather_line()
    down.gather_line()
    tail.scatter()
    up.gather_second()
    down.gather_second()
    tail.middle()
    up.gather()
    down.gather()
    tail.gather()
    up.gather_pair()
    down.gather_pair()
    up.finish()
    down.finish()
    leave(up_total, o_gup)
    for j in range(4):
        leave(down_total.at[:, :, 256 * j : 256 * j + 256], o_gdown.at[:, j])
    tail.gather_pair()
    tail.finish()
    leave(tail_total.at[:, :, OUT : OUT + 256], o_gout)
    leave(tail_total.at[:, :, GX : GX + 256], o_gx)
    leave(tail_total.at[:, :, GFX : GFX + 256], o_gfx)

    gs = tail_total[0:4, :, rest[0] : rest[1]].reshape(32, 128)
    o_gslice[...] = (gs + pltpu.roll(gs, SLICES, 1))[:, :SLICES]
    ga = tail_total[4:8, :, rest[0] : rest[1]].reshape(32, 128)
    o_gada[...] = row_of(jnp.sum(ga, axis=1, keepdims=True))
    gb = jnp.concatenate([tail_total[9, i : i + 1, rest[0] : rest[1]] for i in range(4)], axis=1)
    gb = gb * (-inv_base)
    pick = iota((HEADS, LANES), 0) == iota((HEADS, LANES), 1) // SLICES
    gb = jnp.sum(jnp.where(pick, jnp.broadcast_to(gb, (HEADS, LANES)), 0.0), axis=1, keepdims=True)
    o_gbase[...] = row_of(gb)
    for i in range(2):
        o_ggain1[:, 128 * i : 128 * i + 128] = tail_total[10, i : i + 1, rest[0] : rest[1]]
        o_ggain2[:, 128 * i : 128 * i + 128] = tail_total[10, i + 2 : i + 3, rest[0] : rest[1]]
    for i in range(8):
        o_gbup[:, 128 * i : 128 * i + 128] = tail_total[8, i : i + 1, rest[0] : rest[1]]
    for c in leaving:
        c.wait()


def write_out(*refs):
    count = len(refs) // 3
    sems = refs[-1]
    ins, outs, held = refs[:count], refs[count : 2 * count], refs[2 * count : 3 * count]
    arriving = [pltpu.make_async_copy(ins[i], held[i], sems.at[0, i]) for i in range(count)]
    leaving = [pltpu.make_async_copy(held[i], outs[i], sems.at[1, i]) for i in range(count)]
    for c in arriving:
        c.start()
    for a, c in zip(arriving, leaving):
        a.wait()
        c.start()
    for c in leaving:
        c.wait()


def deep_buffers():
    shapes = [(32, 8, 1024), (16, 8, 1024), (4, 4, 8, 1024), (4, 8, 1024), *((8, 8, 128),) * 3, (32, 8, 1024)]
    return [(shape, F32) for shape in shapes]


def wide_buffers(columns, first, second, per):
    return [
        (shape + (8, columns), F32) for shape in ((32,), (16,), (first, per), (second, per), (32,))
    ]


def per_device(*args):
    (points, cot, gain1, w_x, w_fx, w_slice, base, ada, wq, wk, wv, w_out, gain2, w_up, b_up, w_down) = args
    row = lambda v: v.reshape(1, -1)
    ins = (
        points, cot, row(gain1), w_x, w_fx, w_slice, row(base), row(ada), wq, wk, wv, w_out, row(gain2), w_up,
        row(b_up), w_down,
    )
    spec = pl.BlockSpec(memory_space=pltpu.VMEM)
    outs = [
        ((N, C), BF16), ((1, C), F32), ((32, 8, 256), F32), ((32, 8, 256), F32), ((HEAD_DIM, SLICES), F32),
        ((1, HEADS), F32), ((1, HEAD_DIM), F32), ((32, 32), F32), ((32, 32), F32), ((32, 32), F32),
        ((32, 8, 256), F32), ((1, C), F32), ((32, 8, 1024), F32), ((1, HIDDEN), F32), ((32, 4, 8, 256), F32),
    ]
    large = (0, 2, 3, 10, 12, 14)
    held = [
        ((N, C), BF16), ((N, C), F32), ((N, 1), F32), ((N, C), BF16), ((N, C), BF16), ((N, LANES), F32),
        ((N, LANES), BF16), ((N, LANES), F32), ((N, LANES), F32), ((N, LANES), F32),
        ((8, C), F32), ((8, 1), F32), ((N, C), BF16), ((N, HIDDEN), BF16), ((N, HIDDEN), BF16), ((N, HIDDEN), F32),
        ((N, C), BF16), ((N, C), F32), ((N, C), BF16), ((N, C), BF16), ((N, LANES), F32), ((N, C), BF16),
        ((N, C), BF16), ((N, LANES), BF16), ((N, LANES), BF16),
        ((C, 2 * LANES), BF16), ((C, 2 * LANES), BF16), ((256, 256), BF16), ((C, LANES), F32), ((C, LANES), BF16), ((C, LANES), BF16),
        ((C, LANES), BF16), ((C, LANES), BF16), ((1, LANES), F32), ((1, HIDDEN), F32), ((1, C), F32), ((1, C), F32), ((1, LANES), F32),
        ((C, LANES), F32), ((4, 128, 128), F32),
        *(((16, 9, 128), F32),) * 4, *(((16, 8, 128), F32),) * 4,
        *deep_buffers(), *deep_buffers(), *wide_buffers(TAIL, 16, 8, 1),
    ]
    sems = [pltpu.SemaphoreType.DMA((k, 16)) for k in (6, 6, 16, 16, 10)]
    sems += [pltpu.SemaphoreType.DMA((9,)), pltpu.VMEM((N, C), BF16)]
    sems += [pltpu.VMEM((C, N), BF16)] * 3 + [pltpu.VMEM((TILE, HIDDEN), F32), pltpu.VMEM((TILE, LANES), F32)]
    anywhere = pl.BlockSpec(memory_space=pl.ANY)
    got = pl.pallas_call(
        kernel,
        out_shape=[jax.ShapeDtypeStruct(s, d) for s, d in outs],
        in_specs=[spec] * len(ins),
        out_specs=[anywhere if i in large else spec for i in range(len(outs))],
        scratch_shapes=[pltpu.VMEM(s, d) for s, d in held] + sems,
        compiler_params=pltpu.CompilerParams(
            collective_id=1, has_side_effects=True, vmem_limit_bytes=60 << 20
        ),
    )(*ins)
    got = pl.pallas_call(
        write_out,
        out_shape=[jax.ShapeDtypeStruct(s, d) for s, d in outs],
        in_specs=[anywhere] * len(outs),
        out_specs=[anywhere] * len(outs),
        scratch_shapes=[pltpu.VMEM(s, d) for s, d in outs] + [pltpu.SemaphoreType.DMA((2, len(outs)))],
    )(*got)
    shapes = (
        (N, C), (C,), (C, C), (C, C), (HEAD_DIM, SLICES), (HEADS,), (HEAD_DIM,), (32, 32), (32, 32), (32, 32), (C, C),
        (C,), (C, HIDDEN), (HIDDEN,), (HIDDEN, C),
    )
    return tuple(g.reshape(s) for g, s in zip(got, shapes))


def solution(mesh):
    rows, whole = P("pts", None), P()
    return jax.shard_map(
        per_device,
        mesh=mesh,
        in_specs=(rows, rows) + (whole,) * 14,
        out_specs=(rows,) + (whole,) * 14,
        check_vma=False,
    )
```
